256 devices in a mesh: node: 16 (over x, y), local: 16 (over z, core).
Axes of the slice: x: 4, y: 4, z: 8, core: 2. Of those that a mesh axis runs over, the one named last changes fastest.
Arguments:
- pooled: bfloat16 [131072, 512], P(('node', 'local')), may hold values from -6 to 6
- lookups: int32 [131072, 4], P(('node', 'local')), may hold values from 0 to 16895, as said below
- converted: int32 [131072], P(('node', 'local')), may hold values 0 or 1
- w_hidden: bfloat16 [512, 2048], replicated, may hold values from -0.25 to 0.25
- w_out: bfloat16 [2048], replicated, may hold values from -0.125 to 0.125
- hot_accum: float32 [4, 512, 128], replicated, may hold values from 0.01 to 1
- cold_accum: float32 [4, 16384, 128], P(None, ('node', 'local')), may hold values from 1e-05 to 0.01
Outputs:
- w1_grad: bfloat16 [512, 2048], replicated
- hot_step: float32 [4, 512, 128], replicated
- cold_step: float32 [4, 16384, 128], P(None, ('node', 'local'))
The draws below stay inside these ranges and needn't reach their ends.
Inputs may be any that keep to these rules, and one draw needn't show every extreme that they name: `lookups`: each entry below 512 names a hot row of its table; an entry 512 + c names cold row c of its table, held by device c // 64 (device index node * 16 + local). Among the 512 samples of one device, at most 8 entries over all tables name cold rows of one owner; in every draw some owner receives exactly 8 from every device.
All inputs are finite; a program needn't handle non-finite values. No bound on the sum of `converted` on one device may be relied on, other than what follows from the above.
Results may differ from the reference program's by a relative error of at most 0.0066.
Values may be sent and summed in bfloat16 or wider, within the bound.
No kernel may reach another device: no remote copies, remote signals or barrier semaphores. Data moves between devices by JAX's collectives and lax.ppermute only.
A program may use at most 64 MiB of HBM per device.

```python
import math
import jax
import jax.numpy as jnp
from jax import lax

E = 128
HID = 2048
TABLES = 4
HOT = 512
COLD_DEV = 64
CAP = 8
TOK_DEV = 512
FEAT = 512
TOKENS = 131072
COLD = 16384


def draw_lookups(key, part):
    key = jax.random.fold_in(key, 11)
    owners = TOKENS // TOK_DEV
    busiest = jax.random.randint(jax.random.fold_in(key, 1), (), 0, owners)
    device_keys = jax.random.split(jax.random.fold_in(key, 2), owners)

    def one_device(dev_key):
        key_count, key_row, key_hot, key_perm = jax.random.split(dev_key, 4)
        counts = jax.random.randint(key_count, (owners,), 0, CAP + 1)
        counts = jnp.where(jnp.arange(owners, dtype=jnp.int32) == busiest, CAP, counts)
        slot_index = jnp.arange(owners * CAP, dtype=jnp.int32)
        owner_ids = slot_index // CAP
        is_live = slot_index % CAP < counts[owner_ids]
        local_row = jax.random.randint(key_row, (owners * CAP,), 0, COLD_DEV)
        cold_ids = HOT + owner_ids * COLD_DEV + local_row
        hot_ids = jax.random.randint(key_hot, (TOK_DEV * TABLES,), 0, HOT)
        places = jax.random.permutation(key_perm, TOK_DEV * TABLES)[:owners * CAP]
        chosen = jnp.where(is_live, cold_ids, hot_ids[places])
        return hot_ids.at[places].set(chosen).reshape(TOK_DEV, TABLES)
    return jax.vmap(one_device)(device_keys).reshape(TOKENS, TABLES).astype(jnp.int32)


def plant(drawn, key, smallest, top_value):
    longest = drawn.shape.index(max(drawn.shape))
    spots = []
    for shift in (0, 1):
        where = [jax.random.randint(jax.random.fold_in(key, axis), (), 0, length) for axis, length in enumerate(drawn.shape)]
        where[longest] = (where[longest] + shift) % drawn.shape[longest]
        spots.append(tuple(where))
    return drawn.at[spots[0]].set(smallest).at[spots[1]].set(top_value)


def level_of(own_key, shape, shards, smallest, top_value):
    factor_of, own = 1.0, jax.random.fold_in(own_key, 6)
    for position, shards_of in shards:
        steps = jnp.exp(jax.random.uniform(jax.random.fold_in(own, position), (shards_of,), jnp.float32, smallest / len(shards), top_value / len(shards)))
        factor_of = factor_of * jnp.repeat(steps, shape[position] // shards_of).reshape([-1 if axis == position else 1 for axis in range(len(shape))])
    return factor_of


def gaussian(stream_key, shape, spread, reach, cuts=(), held_as=jnp.bfloat16):
    entries = jax.random.normal(stream_key, shape, jnp.float32) * spread
    if len(cuts) > 0:
        entries = level_of(stream_key, shape, cuts, -0.22, 0.18) * entries
    return jnp.clip(entries, min=-reach, max=reach).astype(held_as)


def setup_inputs(seed: int = 0) -> dict:
    splits = jax.random.split(jax.random.key(seed), 8)
    pooled = gaussian(splits[0], (TOKENS, FEAT), 1.0, 6.0, ((0, 256),))
    lookups = draw_lookups(jax.random.fold_in(splits[7], 71), 0)
    converted = plant((jax.random.randint(splits[2], (TOKENS,), 0, 4) < 1).astype(jnp.int32), jax.random.fold_in(splits[2], 1), 0, 1)
    w_hidden = gaussian(splits[3], (FEAT, HID), FEAT ** -0.5, 0.25)
    w_out = gaussian(splits[4], (HID,), HID ** -0.5, 0.125)
    hot_accum = jnp.clip(jnp.exp(jax.random.uniform(splits[5], (TABLES, HOT, E), jnp.float32, math.log(0.01), math.log(1.0))), 0.01, 1.0)
    cold_accum = jnp.clip(jnp.exp(math.log(0.01) - 6.9077553 * jax.random.uniform(splits[6], (TABLES, COLD, E), jnp.float32) ** level_of(splits[6], (TABLES, COLD, E), ((1, 256),), -0.2, 0.2)), 9.999999747378752e-06, 0.01)
    return {"pooled": pooled, "lookups": lookups, "converted": converted, "w_hidden": w_hidden, "w_out": w_out, "hot_accum": hot_accum, "cold_accum": cold_accum}


def silu_grad(values):
    sig = jax.nn.sigmoid(values)
    return sig * (1.0 + values * (1.0 - sig))

def backprop(rows_x, rows_label, w_hidden, w_out):
    pre_act = jnp.dot(rows_x, w_hidden, preferred_element_type=jnp.float32)
    hidden = jax.nn.silu(pre_act).astype(jnp.bfloat16)
    logit = jnp.dot(hidden, w_out, preferred_element_type=jnp.float32)
    chance = jax.nn.sigmoid(logit)
    target_value = rows_label.astype(jnp.float32)
    loss_weight = target_value * (1.0 + chance) + (1.0 - target_value) * (1.0 - chance) * (1.0 + chance)
    logit_grad = loss_weight * (chance - target_value)
    pre_grad = (logit_grad[:, None] * w_out.astype(jnp.float32)[None, :] * silu_grad(pre_act)).astype(jnp.bfloat16)
    input_grad = lax.dot_general(pre_grad, w_hidden, (((1,), (1,)), ((), ())), preferred_element_type=jnp.float32).astype(jnp.bfloat16)
    weight_term = lax.dot_general(rows_x, pre_grad, (((0,), (0,)), ((), ())), preferred_element_type=jnp.float32)
    return (input_grad, weight_term)

def reference(pooled, lookups, converted, w_hidden, w_out, hot_accum, cold_accum):
    block_count = TOKENS // TOK_DEV
    pieces = (pooled.reshape(block_count, TOK_DEV, FEAT), lookups.reshape(block_count, TOK_DEV, TABLES), converted.reshape(block_count, TOK_DEV))

    def scan_block(totals, piece):
        w1_total, hot_total, cold_total = totals
        rows_x, rows_ids, rows_label = piece
        input_grad, weight_term = backprop(rows_x, rows_label, w_hidden, w_out)
        grads3 = input_grad.reshape(TOK_DEV, TABLES, E).astype(jnp.float32)
        onehot = (rows_ids[:, :, None] == jnp.arange(HOT, dtype=jnp.int32)[None, None, :]).astype(jnp.float32)
        hot_total = hot_total + jnp.einsum('bth,bte->the', onehot, grads3)
        is_cold = rows_ids >= HOT
        target = jnp.arange(TABLES, dtype=jnp.int32)[None, :] * COLD + rows_ids - HOT
        target = jnp.where(is_cold, target, TABLES * COLD).astype(jnp.int32)
        cold_total = cold_total.at[target.reshape(-1)].add(grads3.reshape(-1, E), mode='drop')
        return ((w1_total + weight_term, hot_total, cold_total), None)
    start = (jnp.zeros((FEAT, HID), jnp.float32), jnp.zeros((TABLES, HOT, E), jnp.float32), jnp.zeros((TABLES * COLD, E), jnp.float32))
    totals, unused = lax.scan(scan_block, start, pieces)
    w1_total, hot_sum, cold_flat = totals
    cold_sum = cold_flat.reshape(TABLES, COLD, E)
    hot_step = hot_sum / jnp.sqrt(hot_accum + hot_sum * hot_sum)
    cold_step = cold_sum / jnp.sqrt(cold_accum + cold_sum * cold_sum)
    return (w1_total.astype(jnp.bfloat16), hot_step, cold_step)
```

```python
import functools

import jax
import jax.numpy as jnp
from jax import lax
from jax.experimental import pallas as pl
from jax.experimental.pallas import tpu as pltpu
from jax.sharding import PartitionSpec as P

CAP = 8
E = 128
HID = 2048
FEAT = 512
TOK = 512
TABLES = 4
HOT = 512
COLD_DEV = 64
NODES = 16
LOCALS = 16
ZS = 8
OWNERS = NODES * LOCALS
HALF = FEAT // 2
WIDE = HID + 512
CHUNK = HALF // NODES
ZCOL = HID // ZS
ZWIDE = ZCOL + E
SLOTS = LOCALS * CAP
SLAB = SLOTS + 16
BF = jnp.bfloat16
F32 = jnp.float32
LIMIT = pltpu.CompilerParams(vmem_limit_bytes=56 * 1024 * 1024)


def dot(a, b):
    return jnp.dot(a, b, preferred_element_type=F32)


def dot_nt(a, b):
    return lax.dot_general(a, b, (((1,), (1,)), ((), ())), preferred_element_type=F32)


def wide(tile, copies):
    return jnp.concatenate([tile] * copies, axis=1)


def backprop_kernel(core_ref, x_ref, ids_ref, y_ref, wh_ref, wo_ref, send_ref, own_ref, grad_ref, slope_ref, pre_ref, xt_ref):
    core = core_ref[0]
    step = 256
    x = x_ref[...]
    logit = jnp.zeros((TOK, E), F32)
    for j in range(HID // step):
        cols = slice(j * step, (j + 1) * step)
        v = dot(x, wh_ref[:, cols])
        s = jax.nn.sigmoid(v)
        h = v * s
        slope_ref[:, cols] = s + h * (1.0 - s)
        out_row = jnp.broadcast_to(wo_ref[:, cols], (E, step))
        logit = logit + dot_nt(h.astype(BF), out_row)
    xt_ref[...] = x.T
    chance = jax.nn.sigmoid(logit)
    y = jnp.broadcast_to(y_ref[...].astype(F32), (E, TOK)).T
    weight = y * (1.0 + chance) + (1.0 - y) * (1.0 - chance) * (1.0 + chance)
    lg = wide(weight * (chance - y), step // E)
    own_rows = pl.ds(pl.multiple_of(core * HALF, HALF), HALF)
    far_rows = pl.ds(pl.multiple_of((1 - core) * HALF, HALF), HALF)
    for j in range(HID // step):
        cols = slice(j * step, (j + 1) * step)
        out_row = wo_ref[:, cols].astype(F32)
        pre = (lg * out_row * slope_ref[:, cols]).astype(BF)
        pre_ref[:, cols] = pre
        send_ref[:, cols] = dot(xt_ref[far_rows, :], pre).astype(BF)
        own_ref[:, cols] = dot(xt_ref[own_rows, :], pre).astype(BF)
    grad_ref[...] = dot_nt(pre_ref[...], wh_ref[...]).astype(BF)
    hot_iota = lax.broadcasted_iota(jnp.int32, (HOT, TOK), 0)
    for side, out_ref in ((1 - core, send_ref), (core, own_ref)):
        for t in range(2):
            table = side * 2 + t
            hit = ids_ref[pl.ds(table, 1), :] == hot_iota
            onehot = jnp.where(hit, 1.0, 0.0).astype(BF)
            grads = grad_ref[:, pl.ds(pl.multiple_of(table * E, E), E)]
            total = dot(onehot, grads).astype(BF)
            at = HID + 2 * t * E
            out_ref[:, at:at + E] = total[:HALF]
            out_ref[:, at + E:at + 2 * E] = total[HALF:]


def backprop(core, x, ids, y, wh, wo):
    vmem = pl.BlockSpec(memory_space=pltpu.VMEM)
    half = jax.ShapeDtypeStruct((HALF, WIDE), BF)
    return pl.pallas_call(
        backprop_kernel,
        out_shape=(half, half, jax.ShapeDtypeStruct((TOK, FEAT), BF)),
        in_specs=[pl.BlockSpec(memory_space=pltpu.SMEM)] + [vmem] * 5,
        out_specs=(vmem, vmem, vmem),
        scratch_shapes=[
            pltpu.VMEM((TOK, HID), F32),
            pltpu.VMEM((TOK, HID), BF),
            pltpu.VMEM((FEAT, TOK), BF),
        ],
        compiler_params=LIMIT,
    )(core, x, ids, y, wh, wo)


def pack_kernel(ids_ref, grad_ref, out_ref, rows_ref):
    owner_iota = lax.broadcasted_iota(jnp.int32, (OWNERS, TOK), 0)
    earlier = lax.broadcasted_iota(jnp.int32, (TOK, TOK), 0) < lax.broadcasted_iota(jnp.int32, (TOK, TOK), 1)
    earlier = jnp.where(earlier, 1.0, 0.0).astype(BF)
    carry = jnp.zeros((OWNERS, 1), F32)
    slots, names = [], []
    for t in range(TABLES):
        ids = ids_ref[t:t + 1, :]
        cold = ids >= HOT
        offset = jnp.where(cold, ids - HOT, 0)
        owner = jnp.where(cold, offset >> 6, -1)
        member = jnp.where(owner == owner_iota, 1.0, 0.0)
        before = dot(member.astype(BF), earlier) + carry
        rank = jnp.sum(member * before, axis=0, keepdims=True).astype(jnp.int32)
        carry = carry + jnp.sum(member, axis=1, keepdims=True)
        slot = ((owner & (LOCALS - 1)) * NODES + (owner >> 4)) * CAP + rank
        slots.append(jnp.where(cold, slot, -1))
        names.append((offset & (COLD_DEV - 1)) + t * COLD_DEV)
        rows_ref[t * TOK:(t + 1) * TOK, :] = grad_ref[:, t * E:(t + 1) * E]
    slot_col = jnp.concatenate(slots + slots, axis=0).astype(F32).T.astype(jnp.int32)
    lane = lax.broadcasted_iota(jnp.int32, (TOK, SLOTS), 1)
    group = lax.broadcasted_iota(jnp.int32, (LOCALS, TOK), 0)
    labels = jnp.zeros((LOCALS, SLOTS), F32)
    for t in range(TABLES):
        low = jnp.where((slot_col[:, t:t + 1] & (SLOTS - 1)) == lane, 1.0, 0.0).astype(BF)
        high = jnp.where((slots[t] >> 7) == group, names[t].astype(F32), 0.0).astype(BF)
        labels = labels + dot(high, low)
    labels = labels.astype(BF)
    flat = jnp.concatenate(slots, axis=1)
    block = 512
    per = block // SLOTS
    iota = lax.broadcasted_iota(jnp.int32, (block, TABLES * TOK), 0)
    for b in range(LOCALS // per):
        member = jnp.where(flat - b * block == iota, 1.0, 0.0).astype(BF)
        packed = dot(member, rows_ref[...]).astype(BF)
        for q in range(per):
            out_ref[b * per + q, :SLOTS, :] = packed[q * SLOTS:(q + 1) * SLOTS]
            out_ref[b * per + q, SLOTS:, :] = labels


def pack(ids, grads):
    vmem = pl.BlockSpec(memory_space=pltpu.VMEM)
    return pl.pallas_call(
        pack_kernel,
        out_shape=jax.ShapeDtypeStruct((LOCALS, SLAB, E), BF),
        in_specs=[vmem] * 2,
        out_specs=vmem,
        scratch_shapes=[pltpu.VMEM((TABLES * TOK, E), BF)],
        compiler_params=LIMIT,
    )(ids, grads)


def add_kernel(a_ref, b_ref, out_ref):
    out_ref[...] = (a_ref[...].astype(F32) + b_ref[...].astype(F32)).astype(BF)


def add_halves(a, b):
    vmem = pl.BlockSpec(memory_space=pltpu.VMEM)
    return pl.pallas_call(
        add_kernel,
        out_shape=jax.ShapeDtypeStruct(a.shape, BF),
        in_specs=[vmem] * 2,
        out_specs=vmem,
        compiler_params=LIMIT,
    )(a, b)


def node_sum_kernel(in_ref, out_ref):
    total = in_ref[0].astype(F32)
    for n in range(1, NODES):
        total = total + in_ref[n].astype(F32)
    for z in range(ZS):
        out_ref[z, :, :ZCOL] = total[:, z * ZCOL:(z + 1) * ZCOL].astype(BF)
        at = HID + (z // 2) * E
        row = (z % 2) * 8
        hot = total[row:row + 8, at:at + E]
        hot = jnp.concatenate([hot, jnp.zeros_like(hot)], axis=0)
        out_ref[z, :, ZCOL:] = hot.astype(BF)


def node_sum(parts):
    vmem = pl.BlockSpec(memory_space=pltpu.VMEM)
    return pl.pallas_call(
        node_sum_kernel,
        out_shape=jax.ShapeDtypeStruct((ZS, CHUNK, ZWIDE), BF),
        in_specs=[vmem],
        out_specs=vmem,
        compiler_params=LIMIT,
    )(parts)


def z_sum_kernel(at_ref, in_ref, accum_ref, out_ref):
    total = in_ref[0].astype(F32)
    for z in range(1, ZS):
        total = total + in_ref[z].astype(F32)
    hot = total[:8, ZCOL:]
    stepped = hot / jnp.sqrt(accum_ref[...] + hot * hot)
    stepped = jnp.concatenate([stepped, jnp.zeros_like(stepped)], axis=0)
    done = jnp.concatenate([total[:, :ZCOL], stepped], axis=1).astype(BF)
    for z in range(ZS):
        out_ref[z] = done


def z_sum(block, parts, accum):
    return pl.pallas_call(
        z_sum_kernel,
        out_shape=jax.ShapeDtypeStruct((ZS, CHUNK, ZWIDE), BF),
        grid_spec=pltpu.PrefetchScalarGridSpec(
            num_scalar_prefetch=1,
            grid=(1,),
            in_specs=[
                pl.BlockSpec((ZS, CHUNK, ZWIDE), lambda i, at: (0, 0, 0)),
                pl.BlockSpec((8, E), lambda i, at: (at[0], 0)),
            ],
            out_specs=pl.BlockSpec((ZS, CHUNK, ZWIDE), lambda i, at: (0, 0, 0)),
        ),
        compiler_params=LIMIT,
    )(block, parts, accum)


def spread_kernel(in_ref, out_ref):
    parts = [in_ref[z] for z in range(ZS)]
    pieces = [part[:, :ZCOL] for part in parts]
    for k in range(4):
        pair = [parts[2 * k + q][:, ZCOL:].astype(F32)[:8] for q in range(2)]
        pieces.append(jnp.concatenate(pair, axis=0).astype(BF))
    row = jnp.concatenate(pieces, axis=1)
    for n in range(NODES):
        out_ref[n] = row


def spread(parts):
    vmem = pl.BlockSpec(memory_space=pltpu.VMEM)
    return pl.pallas_call(
        spread_kernel,
        out_shape=jax.ShapeDtypeStruct((NODES, CHUNK, WIDE), BF),
        in_specs=[vmem],
        out_specs=vmem,
        compiler_params=LIMIT,
    )(parts)


def finish_kernel(core_ref, own_ref, far_ref, w1_ref, hot_ref):
    core = core_ref[0]
    for side, in_ref in ((core, own_ref), (1 - core, far_ref)):
        w1_ref[pl.ds(pl.multiple_of(side * HALF, HALF), HALF), :] = in_ref[:, :HID]
        for k in range(4):
            row = pl.multiple_of(side * 1024 + k * HALF, HALF)
            hot_ref[pl.ds(row, HALF), :] = in_ref[:, HID + k * E:HID + (k + 1) * E].astype(F32)


def finish(core, own, far):
    vmem = pl.BlockSpec(memory_space=pltpu.VMEM)
    return pl.pallas_call(
        finish_kernel,
        out_shape=(
            jax.ShapeDtypeStruct((FEAT, HID), BF),
            jax.ShapeDtypeStruct((TABLES * HOT, E), F32),
        ),
        in_specs=[pl.BlockSpec(memory_space=pltpu.SMEM), vmem, vmem],
        out_specs=(vmem, vmem),
        compiler_params=LIMIT,
    )(core, own, far)


def cold_kernel(node_ref, in_ref, accum_ref, out_ref):
    node = node_ref[0]
    labels = jnp.concatenate([in_ref[n, SLOTS:, :] for n in range(NODES)], axis=0)
    lane = lax.broadcasted_iota(jnp.int32, (SLOTS, SLOTS), 0)
    place = lax.broadcasted_iota(jnp.int32, (SLOTS, SLOTS), 1)
    pick = jnp.where(lane == node * CAP + (place & (CAP - 1)), 1.0, 0.0).astype(BF)
    moved = dot(labels, pick)
    keep = lax.broadcasted_iota(jnp.int32, (LOCALS, SLOTS), 0) == lax.broadcasted_iota(jnp.int32, (LOCALS, SLOTS), 1) >> 3
    rows = lax.broadcasted_iota(jnp.int32, (TABLES * COLD_DEV, SLOTS), 0).astype(F32)
    total = jnp.zeros((TABLES * COLD_DEV, E), F32)
    for n in range(NODES):
        named = jnp.where(keep, moved[n * LOCALS:(n + 1) * LOCALS], 0.0)
        named = jnp.sum(named, axis=0, keepdims=True)
        onehot = jnp.where(named == rows, 1.0, 0.0).astype(BF)
        total = total + dot(onehot, in_ref[n, :SLOTS, :])
    accum = accum_ref[...]
    out_ref[...] = total / jnp.sqrt(accum + total * total)


def cold_update(node, arrived, accum):
    vmem = pl.BlockSpec(memory_space=pltpu.VMEM)
    return pl.pallas_call(
        cold_kernel,
        out_shape=jax.ShapeDtypeStruct((TABLES * COLD_DEV, E), F32),
        in_specs=[pl.BlockSpec(memory_space=pltpu.SMEM), vmem, vmem],
        out_specs=vmem,
        compiler_params=LIMIT,
    )(node, arrived, accum)


def on_device(pooled, lookups, converted, w_hidden, w_out, hot_accum, cold_accum):
    node = lax.axis_index("node")
    local = lax.axis_index("local")
    zed, core = local // 2, local % 2
    ids = lookups.T
    core_arg = core.reshape(1)
    swap = [(i, i ^ 1) for i in range(LOCALS)]
    same_core = [[2 * z + c for z in range(ZS)] for c in range(2)]
    send, own, grads = backprop(
        core_arg, pooled, ids, converted.reshape(1, TOK), w_hidden, w_out.reshape(1, HID)
    )
    other = lax.ppermute(send, "local", swap)
    slab = pack(ids, grads)
    chip = add_halves(own, other)
    parts = lax.all_to_all(chip.reshape(NODES, CHUNK, WIDE), "node", 0, 0, tiled=True)
    slab = lax.all_to_all(slab, "local", 0, 0, tiled=True)
    rows = slab[:, :SLOTS].reshape(LOCALS, NODES, CAP, E).transpose(1, 0, 2, 3)
    labels = lax.dynamic_index_in_dim(slab, SLOTS + local, 1, keepdims=False)
    slab = jnp.concatenate(
        [
            rows.reshape(NODES, SLOTS, E),
            jnp.broadcast_to(labels[None], (NODES, LOCALS, E)),
        ],
        axis=1,
    )
    parts = lax.all_to_all(node_sum(parts), "local", 0, 0, axis_index_groups=same_core, tiled=True)
    block = (core * 1024 + (zed // 2) * HALF + node * CHUNK + (zed % 2) * 8) // 8
    parts = z_sum(block.reshape(1), parts, hot_accum.reshape(TABLES * HOT, E))
    slab = lax.all_to_all(slab, "node", 0, 0, tiled=True)
    parts = lax.all_to_all(parts, "local", 0, 0, axis_index_groups=same_core, tiled=True)
    parts = lax.all_to_all(spread(parts), "node", 0, 0, tiled=True)
    half = parts.reshape(HALF, WIDE)
    far = lax.ppermute(half, "local", swap)
    w1_grad, hot_step = finish(core_arg, half, far)
    cold_step = cold_update(node.reshape(1), slab, cold_accum.reshape(TABLES * COLD_DEV, E))
    return (w1_grad, hot_step.reshape(TABLES, HOT, E), cold_step.reshape(TABLES, COLD_DEV, E))


def solution(mesh):
    both = ("node", "local")
    in_specs = (P(both, None), P(both, None), P(both), P(), P(), P(), P(None, both, None))
    out_specs = (P(), P(), P(None, both, None))
    return jax.shard_map(on_device, mesh=mesh, in_specs=in_specs, out_specs=out_specs, check_vma=False)
```

```python
import jax
import jax.numpy as jnp
from jax import lax
from jax.experimental import pallas as pl
from jax.experimental.pallas import tpu as pltpu
from jax.sharding import Mesh
from jax.sharding import PartitionSpec as P

CAP = 8
E = 128
HID = 2048
FEAT = 512
TOK = 512
TABLES = 4
HOT = 512
COLD_DEV = 64
NODES = 16
LOCALS = 16
ZQ = 4
ZP = 2
GROUP = NODES * ZP
OWNERS = NODES * LOCALS
HALF = FEAT // 2
CHUNK = HALF // NODES
PCOL = HID // ZP
WIDE = PCOL + 2 * E
HOT_HALF = TABLES * HOT // 2
SLOT_HALF = OWNERS * CAP // 2
NODE_SLOTS = SLOT_HALF // NODES
PAIR = 2 * CAP
SLAB = ZQ + 1
BF = jnp.bfloat16
F32 = jnp.float32
MIB = 1024 * 1024
AXES = ("node", "zq", "zp", "core")
VMEM = pl.BlockSpec(memory_space=pltpu.VMEM)
HBM = pl.BlockSpec(memory_space=pltpu.HBM)
SMEM = pl.BlockSpec(memory_space=pltpu.SMEM)


def dot(a, b):
    return jnp.dot(a, b, preferred_element_type=F32)


def dot_nt(a, b):
    return lax.dot_general(a, b, (((1,), (1,)), ((), ())), preferred_element_type=F32)


def shape(*dims, dtype=BF):
    return jax.ShapeDtypeStruct(dims, dtype)


def call(kernel, out_shape, args, scalars=0, scratch=(), limit=16, flops=0, size=0, spec=VMEM, out_specs=None):
    many = isinstance(out_shape, (tuple, list))
    return pl.pallas_call(
        kernel,
        out_shape=out_shape,
        in_specs=[SMEM] * scalars + [spec] * (len(args) - scalars),
        out_specs=out_specs or (tuple(VMEM for _ in out_shape) if many else VMEM),
        scratch_shapes=scratch,
        compiler_params=pltpu.CompilerParams(vmem_limit_bytes=limit * MIB),
        cost_estimate=pl.CostEstimate(flops=flops, bytes_accessed=size, transcendentals=0),
    )(*args)


def backprop_kernel(
    core_ref, x_hbm, ids_hbm, y_hbm, wh_hbm, wo_hbm, send_hbm, own_ref, grad_hbm,
    slope_ref, pre_ref, xt_ref, x_ref, ids_ref, y_ref, wh_ref, wo_ref, send_ref, grad_ref, hit_ref, sems, out_sems,
):
    core = core_ref[0]
    step = 256
    blocks = HID // step
    loads = [
        pltpu.make_async_copy(wh_hbm.at[:, pl.ds(j * step, step)], wh_ref.at[:, pl.ds(j * step, step)], sems.at[j])
        for j in range(blocks)
    ]
    small = [
        pltpu.make_async_copy(src, dst, sems.at[blocks + i])
        for i, (src, dst) in enumerate(((x_hbm, x_ref), (wo_hbm, wo_ref), (ids_hbm, ids_ref), (y_hbm, y_ref)))
    ]
    stores = []

    def store(src, dst):
        copy = pltpu.make_async_copy(src, dst, out_sems.at[len(stores)])
        copy.start()
        stores.append(copy)

    for copy in (*small[1:], small[0], *loads):
        copy.start()
    for copy in small[1:]:
        copy.wait()
    hot_iota = lax.broadcasted_iota(jnp.int32, (HOT, TOK), 0)
    for t in range(TABLES):
        hit = ids_ref[t:t + 1, :] == hot_iota
        hit_ref[t] = jnp.where(hit, 1.0, 0.0).astype(BF)
    small[0].wait()
    x = x_ref[...]
    xt_ref[...] = x.T
    wo = wo_ref[...].astype(F32)
    logit = jnp.zeros((TOK, E), F32)
    for j in range(blocks):
        if j % 4 == 0:
            for copy in loads[j:j + 4]:
                copy.wait()
        cols = slice(j * step, (j + 1) * step)
        v = dot(x, wh_ref[:, cols])
        s = jax.nn.sigmoid(v)
        h = v * s
        slope_ref[:, cols] = s + h * (1.0 - s)
        out_row = jnp.concatenate([wo[2 * j:2 * j + 1], wo[2 * j + 1:2 * j + 2]], axis=1)
        out_row = jnp.broadcast_to(out_row, (E, step)).astype(BF)
        logit = logit + dot_nt(h.astype(BF), out_row)
    chance = jax.nn.sigmoid(logit)
    y = jnp.broadcast_to(y_ref[...].astype(F32), (E, TOK)).T
    weight = y * (1.0 + chance) + (1.0 - y) * (1.0 - chance) * (1.0 + chance)
    lg = weight * (chance - y)
    lg = jnp.concatenate([lg] * (step // E), axis=1)
    own_rows = pl.ds(pl.multiple_of(core * HALF, HALF), HALF)
    far_rows = pl.ds(pl.multiple_of((1 - core) * HALF, HALF), HALF)
    for j in range(HID // step):
        cols = slice(j * step, (j + 1) * step)
        out_row = jnp.concatenate([wo[2 * j:2 * j + 1], wo[2 * j + 1:2 * j + 2]], axis=1)
        pre = (lg * out_row * slope_ref[:, cols]).astype(BF)
        pre_ref[:, cols] = pre
        part, at = divmod(j * step, PCOL)
        for rows, out_ref in ((far_rows, send_ref), (own_rows, own_ref)):
            term = dot(xt_ref[rows, :], pre).astype(BF)
            out_ref[:, part, :, at:at + step] = term.reshape(NODES, CHUNK, step)
        if at + step == PCOL:
            store(send_ref.at[:, part, :, pl.ds(0, PCOL)], send_hbm.at[:, part, :, pl.ds(0, PCOL)])
    grad_ref[...] = dot_nt(pre_ref[...], wh_ref[...]).astype(BF)
    store(grad_ref, grad_hbm)
    for side, out_ref in ((1 - core, send_ref), (core, own_ref)):
        for t in range(ZP):
            table = side * 2 + t
            onehot = hit_ref[table]
            grads = grad_ref[:, pl.ds(pl.multiple_of(table * E, E), E)]
            total = dot(onehot, grads).astype(BF)
            for b in range(2):
                at = PCOL + b * E
                out_ref[:, t, :, at:at + E] = total[b * HALF:(b + 1) * HALF].reshape(NODES, CHUNK, E)
        if out_ref is send_ref:
            store(send_ref.at[:, :, :, pl.ds(PCOL, 2 * E)], send_hbm.at[:, :, :, pl.ds(PCOL, 2 * E)])
    for copy in stores:
        copy.wait()


def pack_kernel(core_ref, ids_ref, grad_ref, send_ref, own_ref, rows_ref):
    core = core_ref[0]
    owner_iota = lax.broadcasted_iota(jnp.int32, (OWNERS, TOK), 0)
    earlier = lax.broadcasted_iota(jnp.int32, (TOK, TOK), 0) < lax.broadcasted_iota(jnp.int32, (TOK, TOK), 1)
    earlier = jnp.where(earlier, 1.0, 0.0).astype(BF)
    carry = jnp.zeros((OWNERS, 1), F32)
    slots, names = [], []
    for t in range(TABLES):
        ids = ids_ref[t:t + 1, :]
        cold = ids >= HOT
        offset = jnp.where(cold, ids - HOT, 0)
        owner = jnp.where(cold, offset >> 6, -1)
        member = jnp.where(owner == owner_iota, 1.0, 0.0)
        before = dot(member.astype(BF), earlier) + carry
        rank = jnp.sum(member * before, axis=0, keepdims=True).astype(jnp.int32)
        carry = carry + jnp.sum(member, axis=1, keepdims=True)
        core_at, zp_at, zq_at, node_at = owner & 1, (owner >> 1) & 1, (owner >> 2) & 3, owner >> 4
        slot = (((core_at * NODES + node_at) * ZP + zp_at) * ZQ + zq_at) * CAP + rank
        slots.append(jnp.where(cold, slot, -1))
        names.append(((offset & (COLD_DEV - 1)) + t * COLD_DEV).astype(F32))
        rows_ref[t * TOK:(t + 1) * TOK, :] = grad_ref[:, t * E:(t + 1) * E]
    slot_col = jnp.concatenate(slots + slots, axis=0).astype(F32).T.astype(jnp.int32)
    lane = lax.broadcasted_iota(jnp.int32, (TOK, E), 1) - core * NODE_SLOTS
    group = lax.broadcasted_iota(jnp.int32, (NODES, TOK), 0)
    flat = jnp.concatenate(slots, axis=1)
    block = 512
    iota = lax.broadcasted_iota(jnp.int32, (block, TABLES * TOK), 0)
    low = [jnp.where((slot_col[:, t:t + 1] & (NODE_SLOTS - 1)) == lane, 1.0, 0.0).astype(BF) for t in range(TABLES)]
    for side, out_ref in ((1 - core, send_ref), (core, own_ref)):
        labels = jnp.zeros((NODES, E), F32)
        for t in range(TABLES):
            high = jnp.where((slots[t] >> 6) - side * NODES == group, names[t], 0.0).astype(BF)
            labels = labels + dot(high, low[t])
        out_ref[SLOT_HALF:, :] = labels.astype(BF)
        for b in range(SLOT_HALF // block):
            member = jnp.where(flat - (side * SLOT_HALF + b * block) == iota, 1.0, 0.0).astype(BF)
            out_ref[b * block:(b + 1) * block, :] = dot(member, rows_ref[...]).astype(BF)


def add_kernel(a_ref, b_ref, out_ref):
    out_ref[...] = a_ref[...] + b_ref[...]


def merge_kernel(core_ref, cold_ref, far_cold_ref, out_ref):
    first = core_ref[0] == 0
    own, far = cold_ref[...].astype(F32), far_cold_ref[...].astype(F32)
    labels = (own[SLOT_HALF:] + far[SLOT_HALF:]).astype(BF)
    own = own[:SLOT_HALF].reshape(GROUP * ZQ, CAP, E)
    far = far[:SLOT_HALF].reshape(GROUP * ZQ, CAP, E)
    pair = [jnp.where(first, own, far), jnp.where(first, far, own)]
    out_ref[:, :ZQ] = jnp.concatenate(pair, axis=1).astype(BF).reshape(GROUP, ZQ, PAIR, E)
    for g in range(GROUP):
        out_ref[g, ZQ] = labels


def group_sum_kernel(in_ref, out_ref):
    total = in_ref[0].astype(F32)
    for g in range(1, GROUP):
        total = total + in_ref[g].astype(F32)
    out_ref[...] = total.astype(BF)


def step_kernel(block_ref, a_ref, b_ref, c_ref, d_ref, accum0_ref, accum1_ref, out_ref):
    total = (a_ref[...].astype(F32) + b_ref[...].astype(F32)) + (c_ref[...].astype(F32) + d_ref[...].astype(F32))
    hot = total[:, PCOL:]
    accum = jnp.concatenate([accum0_ref[...], accum1_ref[...]], axis=1)
    stepped = hot / jnp.sqrt(accum + hot * hot)
    out_ref[...] = jnp.concatenate([total[:, :PCOL], stepped], axis=1).astype(BF)


def spread_kernel(place_ref, own_ref, far_ref, out_ref):
    zp = place_ref[2]
    own, far = own_ref[...], far_ref[...]
    for n in range(NODES):
        out_ref[n, zp] = own
        out_ref[n, 1 - zp] = far


def step(blocks, parts, accum):
    return pl.pallas_call(
        step_kernel,
        out_shape=shape(CHUNK, WIDE),
        grid_spec=pltpu.PrefetchScalarGridSpec(
            num_scalar_prefetch=1,
            grid=(1,),
            in_specs=[VMEM] * ZQ + [
                pl.BlockSpec((CHUNK, E), lambda i, at: (at[0], 0)),
                pl.BlockSpec((CHUNK, E), lambda i, at: (at[1], 0)),
            ],
            out_specs=VMEM,
        ),
        compiler_params=pltpu.CompilerParams(vmem_limit_bytes=16 * MIB),
        cost_estimate=pl.CostEstimate(flops=0, bytes_accessed=2 * MIB, transcendentals=0),
    )(blocks, *parts, accum, accum)


def cold_dense_kernel(place_ref, in_ref, *out_refs):
    node, zq, zp = place_ref[0], place_ref[1], place_ref[2]
    mine = lax.broadcasted_iota(jnp.int32, (NODES, E), 0) == node
    labels = []
    for g in range(GROUP):
        named = jnp.where(mine, in_ref[g, ZQ].astype(F32), 0.0)
        labels.append(jnp.sum(named, axis=0, keepdims=True))
    labels = jnp.concatenate(labels, axis=0).astype(BF)
    entries = GROUP * PAIR
    lane = lax.broadcasted_iota(jnp.int32, (E, entries), 0)
    place = lax.broadcasted_iota(jnp.int32, (E, entries), 1)
    wanted = ((place >> 3) & 1) * NODE_SLOTS + zp * (ZQ * CAP) + (place & 7)
    keep = lax.broadcasted_iota(jnp.int32, (GROUP, entries), 0) == lax.broadcasted_iota(jnp.int32, (GROUP, entries), 1) >> 4
    rows = lax.broadcasted_iota(jnp.int32, (TABLES * COLD_DEV, entries), 0).astype(F32)
    for d, out_ref in enumerate(out_refs):
        target = zq ^ d
        moved = dot(labels, jnp.where(lane == wanted + target * CAP, 1.0, 0.0).astype(BF))
        named = jnp.sum(jnp.where(keep, moved, 0.0), axis=0, keepdims=True)
        onehot = jnp.where(named == rows, 1.0, 0.0).astype(BF)
        out_ref[...] = dot(onehot, in_ref[:, target].reshape(entries, E)).astype(BF)


def cold_step_kernel(accum_ref, a_ref, b_ref, c_ref, d_ref, out_ref):
    total = (a_ref[...].astype(F32) + b_ref[...].astype(F32)) + (c_ref[...].astype(F32) + d_ref[...].astype(F32))
    out_ref[...] = total / jnp.sqrt(accum_ref[...] + total * total)


def finish_kernel(core_ref, in_ref, *refs):
    w1_ref, hot_ref = refs[-2:]
    for part in range(ZP):
        w1_ref[:, part * PCOL:(part + 1) * PCOL] = in_ref[:, part, :, :PCOL].reshape(HALF, PCOL)
        for b in range(2):
            at = PCOL + b * E
            hot = in_ref[:, part, :, at:at + E].reshape(HALF, E)
            hot_ref[(2 * part + b) * HALF:(2 * part + b + 1) * HALF, :] = hot.astype(F32)


def finish(side, half, held=()):
    return pl.pallas_call(
        finish_kernel,
        out_shape=(shape(FEAT, HID), shape(TABLES * HOT, E, dtype=F32)),
        grid_spec=pltpu.PrefetchScalarGridSpec(
            num_scalar_prefetch=1,
            grid=(1,),
            in_specs=[VMEM] + [pl.BlockSpec(memory_space=pl.ANY)] * len(held),
            out_specs=(
                pl.BlockSpec((HALF, HID), lambda i, at: (at[0], 0)),
                pl.BlockSpec((HOT_HALF, E), lambda i, at: (at[0], 0)),
            ),
        ),
        input_output_aliases={2: 0, 3: 1} if held else {},
        compiler_params=pltpu.CompilerParams(vmem_limit_bytes=16 * MIB),
        cost_estimate=pl.CostEstimate(flops=0, bytes_accessed=4 * MIB, transcendentals=0),
    )(side, half, *held)


def on_device(pooled, lookups, converted, w_hidden, w_out, hot_accum, cold_accum):
    node, zq, zp, core = (lax.axis_index(name) for name in AXES)
    ids = lookups.T
    core_arg = core.reshape(1)
    place = jnp.stack([node, zq, zp])

    def in_hbm(array):
        return pltpu.with_memory_space_constraint(array, pltpu.HBM)

    def flip(array, axis, mask):
        return lax.ppermute(array, axis, [(i, i ^ mask) for i in range(lax.axis_size(axis))])

    def exchange(array):
        return lax.all_to_all(array, ("node", "zp"), 0, 0, tiled=True)

    halves = shape(NODES, ZP, CHUNK, WIDE)
    send, own, grads = call(
        backprop_kernel,
        (pltpu.HBM(halves.shape, BF), pltpu.VMEM(halves.shape, BF), pltpu.HBM((TOK, FEAT), BF)),
        (core_arg, *map(in_hbm, (pooled, ids, converted.reshape(1, TOK), w_hidden, w_out.reshape(HID // E, E)))),
        scalars=1,
        scratch=[
            pltpu.VMEM((TOK, HID), F32),
            pltpu.VMEM((TOK, HID), BF),
            pltpu.VMEM((FEAT, TOK), BF),
            pltpu.VMEM((TOK, FEAT), BF),
            pltpu.VMEM((TABLES, TOK), jnp.int32),
            pltpu.VMEM((1, TOK), jnp.int32),
            pltpu.VMEM((FEAT, HID), BF),
            pltpu.VMEM((HID // E, E), BF),
            pltpu.VMEM((NODES, ZP, CHUNK, WIDE), BF),
            pltpu.VMEM((TOK, FEAT), BF),
            pltpu.VMEM((TABLES, HOT, TOK), BF),
            pltpu.SemaphoreType.DMA((HID // 256 + 4,)),
            pltpu.SemaphoreType.DMA((4,)),
        ],
        spec=HBM,
        out_specs=(HBM, VMEM, HBM),
        limit=24,
        flops=4 * 10**9,
        size=8 * MIB,
    )
    chip = call(add_kernel, halves, (own, flip(send, "core", 1)), size=3 * MIB)
    parts = exchange(chip.reshape(GROUP, CHUNK, WIDE))
    cold_send, cold_own = call(
        pack_kernel,
        (shape(SLOT_HALF + NODES, E), shape(SLOT_HALF + NODES, E)),
        (core_arg, ids, grads),
        scalars=1,
        scratch=[pltpu.VMEM((TABLES * TOK, E), BF)],
        flops=6 * 10**9,
        size=8 * MIB,
    )
    slab = call(
        merge_kernel,
        shape(GROUP, SLAB, PAIR, E),
        (core_arg, cold_own, flip(cold_send, "core", 1)),
        scalars=1,
        size=3 * MIB,
    )
    part = call(group_sum_kernel, shape(CHUNK, WIDE), (parts,), size=2 * MIB)
    slab = exchange(slab)
    quad = [part] + [flip(part, "zq", d) for d in range(1, ZQ)]
    block = ((core * ZP + zp) * 2 * HALF + node * CHUNK) // CHUNK
    done = step(jnp.stack([block, block + HALF // CHUNK]), quad, hot_accum.reshape(TABLES * HOT, E))
    whole = call(spread_kernel, halves, (place, done, flip(done, "zp", 1)), scalars=1, size=2 * MIB)
    half = lax.all_to_all(whole, "node", 0, 0, tiled=True)
    cold = call(
        cold_dense_kernel,
        tuple(shape(TABLES * COLD_DEV, E) for _ in range(ZQ)),
        (place, slab),
        scalars=1,
        flops=10**9,
        size=2 * MIB,
    )
    cold = [cold[0]] + [flip(cold[d], "zq", d) for d in range(1, ZQ)]
    half, cold = lax.optimization_barrier((half, cold))
    cold_step = call(
        cold_step_kernel,
        shape(TABLES * COLD_DEV, E, dtype=F32),
        (cold_accum.reshape(TABLES * COLD_DEV, E), *cold),
        size=MIB,
    )
    far = flip(half, "core", 1)
    held = finish(core_arg, half)
    w1_grad, hot_step = finish(1 - core_arg, far, held)
    return (w1_grad, hot_step.reshape(TABLES, HOT, E), cold_step.reshape(TABLES, COLD_DEV, E))


def solution(mesh):
    mesh = Mesh(mesh.devices.reshape(NODES, ZQ, ZP, 2), AXES)
    in_specs = (P(AXES, None), P(AXES, None), P(AXES), P(), P(), P(), P(None, AXES, None))
    out_specs = (P(), P(), P(None, AXES, None))
    return jax.shard_map(on_device, mesh=mesh, in_specs=in_specs, out_specs=out_specs, check_vma=False)
```

```python
import jax
import jax.numpy as jnp
from jax import lax
from jax.experimental import pallas as pl
from jax.experimental.pallas import tpu as pltpu
from jax.sharding import Mesh
from jax.sharding import PartitionSpec as P

CAP = 8
E = 128
HID = 2048
FEAT = 512
TOK = 512
TABLES = 4
HOT = 512
COLD_DEV = 64
NODES = 16
LOCALS = 16
ZQ = 4
ZP = 2
GROUP = NODES * ZP
OWNERS = NODES * LOCALS
HALF = FEAT // 2
CHUNK = HALF // NODES
PCOL = HID // ZP
WIDE = PCOL + 2 * E
HOT_HALF = TABLES * HOT // 2
SLOT_HALF = OWNERS * CAP // 2
NODE_SLOTS = SLOT_HALF // NODES
PAIR = 2 * CAP
SLAB = ZQ + 1
BF = jnp.bfloat16
F32 = jnp.float32
MIB = 1024 * 1024
VMEM = pl.BlockSpec(memory_space=pltpu.VMEM)
HBM = pl.BlockSpec(memory_space=pltpu.HBM)
SMEM = pl.BlockSpec(memory_space=pltpu.SMEM)


def dot(a, b):
    return jnp.dot(a, b, preferred_element_type=F32)


def dot_nt(a, b):
    return lax.dot_general(a, b, (((1,), (1,)), ((), ())), preferred_element_type=F32)


def shape(*dims, dtype=BF):
    return jax.ShapeDtypeStruct(dims, dtype)


def call(kernel, out_shape, args, scalars=0, scratch=(), limit=16, flops=0, size=0, spec=VMEM, out_specs=None):
    many = isinstance(out_shape, (tuple, list))
    return pl.pallas_call(
        kernel,
        out_shape=out_shape,
        in_specs=[SMEM] * scalars + [spec] * (len(args) - scalars),
        out_specs=out_specs or (tuple(VMEM for _ in out_shape) if many else VMEM),
        scratch_shapes=scratch,
        compiler_params=pltpu.CompilerParams(vmem_limit_bytes=limit * MIB),
        cost_estimate=pl.CostEstimate(flops=flops, bytes_accessed=size, transcendentals=0),
    )(*args)


def backprop_kernel(
    core_ref, x_hbm, ids_hbm, y_hbm, wh_hbm, wo_hbm, send_hbm, own_ref, pre_ref, wh_ref, hit_ref,
    slope_ref, xt_ref, x_ref, ids_ref, y_ref, wo_ref, send_ref, sems, out_sems,
):
    core = core_ref[0]
    step = 256
    blocks = HID // step
    loads = [
        pltpu.make_async_copy(wh_hbm.at[:, pl.ds(j * step, step)], wh_ref.at[:, pl.ds(j * step, step)], sems.at[j])
        for j in range(blocks)
    ]
    small = [
        pltpu.make_async_copy(src, dst, sems.at[blocks + i])
        for i, (src, dst) in enumerate(((x_hbm, x_ref), (wo_hbm, wo_ref), (ids_hbm, ids_ref), (y_hbm, y_ref)))
    ]
    stores = []
    for copy in (*small[1:], small[0], *loads):
        copy.start()
    for copy in small[1:]:
        copy.wait()
    hot_iota = lax.broadcasted_iota(jnp.int32, (HOT, TOK), 0)
    for t in range(TABLES):
        hit = ids_ref[t:t + 1, :] == hot_iota
        hit_ref[t] = jnp.where(hit, 1.0, 0.0).astype(BF)
    small[0].wait()
    x = x_ref[...]
    xt_ref[...] = x.T
    wo = wo_ref[...].astype(F32)
    logit = jnp.zeros((TOK, E), F32)
    for j in range(blocks):
        if j % 4 == 0:
            for copy in loads[j:j + 4]:
                copy.wait()
        cols = slice(j * step, (j + 1) * step)
        v = dot(x, wh_ref[:, cols])
        s = jax.nn.sigmoid(v)
        h = v * s
        slope_ref[:, cols] = s + h * (1.0 - s)
        out_row = jnp.concatenate([wo[2 * j:2 * j + 1], wo[2 * j + 1:2 * j + 2]], axis=1)
        out_row = jnp.broadcast_to(out_row, (E, step)).astype(BF)
        logit = logit + dot_nt(h.astype(BF), out_row)
    chance = jax.nn.sigmoid(logit)
    y = jnp.broadcast_to(y_ref[...].astype(F32), (E, TOK)).T
    weight = y * (1.0 + chance) + (1.0 - y) * (1.0 - chance) * (1.0 + chance)
    lg = weight * (chance - y)
    lg = jnp.concatenate([lg] * (step // E), axis=1)
    own_rows = pl.ds(pl.multiple_of(core * HALF, HALF), HALF)
    far_rows = pl.ds(pl.multiple_of((1 - core) * HALF, HALF), HALF)
    for j in range(HID // step):
        cols = slice(j * step, (j + 1) * step)
        out_row = jnp.concatenate([wo[2 * j:2 * j + 1], wo[2 * j + 1:2 * j + 2]], axis=1)
        pre = (lg * out_row * slope_ref[:, cols]).astype(BF)
        pre_ref[:, cols] = pre
        part, at = divmod(j * step, PCOL)
        for rows, out_ref in ((far_rows, send_ref), (own_rows, own_ref)):
            term = dot(xt_ref[rows, :], pre).astype(BF)
            out_ref[:, part, :, at:at + step] = term.reshape(NODES, CHUNK, step)
        if at + step == PCOL:
            copy = pltpu.make_async_copy(send_ref.at[:, part], send_hbm.at[:, part], out_sems.at[part])
            copy.start()
            stores.append(copy)
    for copy in stores:
        copy.wait()


def hot_kernel(core_ref, pre_ref, wh_ref, hit_ref, send_ref, own_ref, grad_ref):
    core = core_ref[0]
    grad_ref[...] = dot_nt(pre_ref[...], wh_ref[...]).astype(BF)
    for side, out_ref in ((1 - core, send_ref), (core, own_ref)):
        for t in range(ZP):
            table = side * 2 + t
            grads = grad_ref[:, pl.ds(pl.multiple_of(table * E, E), E)]
            total = dot(hit_ref[table], grads).astype(BF)
            for b in range(2):
                out_ref[:, t, :, b * E:(b + 1) * E] = total[b * HALF:(b + 1) * HALF].reshape(NODES, CHUNK, E)


def pack_kernel(core_ref, ids_ref, grad_ref, send_ref, own_ref, rows_ref):
    core = core_ref[0]
    owner_iota = lax.broadcasted_iota(jnp.int32, (OWNERS, TOK), 0)
    earlier = lax.broadcasted_iota(jnp.int32, (TOK, TOK), 0) < lax.broadcasted_iota(jnp.int32, (TOK, TOK), 1)
    earlier = jnp.where(earlier, 1.0, 0.0).astype(BF)
    carry = jnp.zeros((OWNERS, 1), F32)
    slots, names = [], []
    for t in range(TABLES):
        ids = ids_ref[t:t + 1, :]
        cold = ids >= HOT
        offset = jnp.where(cold, ids - HOT, 0)
        owner = jnp.where(cold, offset >> 6, -1)
        member = jnp.where(owner == owner_iota, 1.0, 0.0)
        before = dot(member.astype(BF), earlier) + carry
        rank = jnp.sum(member * before, axis=0, keepdims=True).astype(jnp.int32)
        carry = carry + jnp.sum(member, axis=1, keepdims=True)
        core_at, zp_at, zq_at, node_at = owner & 1, (owner >> 1) & 1, (owner >> 2) & 3, owner >> 4
        slot = (((core_at * NODES + node_at) * ZP + zp_at) * ZQ + zq_at) * CAP + rank
        slots.append(jnp.where(cold, slot, -1))
        names.append(((offset & (COLD_DEV - 1)) + t * COLD_DEV).astype(F32))
        rows_ref[t * TOK:(t + 1) * TOK, :] = grad_ref[:, t * E:(t + 1) * E]
    slot_col = jnp.concatenate(slots + slots, axis=0).astype(F32).T.astype(jnp.int32)
    lane = lax.broadcasted_iota(jnp.int32, (TOK, E), 1) - core * NODE_SLOTS
    group = lax.broadcasted_iota(jnp.int32, (NODES, TOK), 0)
    flat = jnp.concatenate(slots, axis=1)
    block = 512
    iota = lax.broadcasted_iota(jnp.int32, (block, TABLES * TOK), 0)
    low = [jnp.where((slot_col[:, t:t + 1] & (NODE_SLOTS - 1)) == lane, 1.0, 0.0).astype(BF) for t in range(TABLES)]
    for side, out_ref in ((1 - core, send_ref), (core, own_ref)):
        labels = jnp.zeros((NODES, E), F32)
        for t in range(TABLES):
            high = jnp.where((slots[t] >> 6) - side * NODES == group, names[t], 0.0).astype(BF)
            labels = labels + dot(high, low[t])
        out_ref[SLOT_HALF:, :] = labels.astype(BF)
        for b in range(SLOT_HALF // block):
            member = jnp.where(flat - (side * SLOT_HALF + b * block) == iota, 1.0, 0.0).astype(BF)
            out_ref[b * block:(b + 1) * block, :] = dot(member, rows_ref[...]).astype(BF)


def add_part(a, b, at, held=None):
    width = a.shape[-1]
    rest = () if held is None else (held,)

    def kernel(a_ref, b_ref, *refs):
        out_hbm, sum_ref, sem = refs[-3:]
        sum_ref[...] = a_ref[...] + b_ref[...]
        copy = pltpu.make_async_copy(sum_ref, out_hbm.at[:, :, :, pl.ds(at, width)], sem)
        copy.start()
        copy.wait()

    return pl.pallas_call(
        kernel,
        out_shape=pltpu.HBM((NODES, ZP, CHUNK, WIDE), BF),
        in_specs=[VMEM] * 2 + [HBM] * len(rest),
        out_specs=HBM,
        scratch_shapes=[pltpu.VMEM(a.shape, BF), pltpu.SemaphoreType.DMA],
        input_output_aliases={2: 0} if rest else {},
        compiler_params=pltpu.CompilerParams(vmem_limit_bytes=8 * MIB),
        cost_estimate=pl.CostEstimate(flops=0, bytes_accessed=2 * MIB, transcendentals=0),
    )(a, b, *rest)


def merge_kernel(core_ref, cold_ref, far_cold_ref, out_ref):
    first = core_ref[0] == 0
    own, far = cold_ref[...].astype(F32), far_cold_ref[...].astype(F32)
    labels = (own[SLOT_HALF:] + far[SLOT_HALF:]).astype(BF)
    own = own[:SLOT_HALF].reshape(GROUP * ZQ, CAP, E)
    far = far[:SLOT_HALF].reshape(GROUP * ZQ, CAP, E)
    pair = [jnp.where(first, own, far), jnp.where(first, far, own)]
    out_ref[:, :ZQ] = jnp.concatenate(pair, axis=1).astype(BF).reshape(GROUP, ZQ, PAIR, E)
    for g in range(GROUP):
        out_ref[g, ZQ] = labels


def group_sum_kernel(in_ref, out_ref):
    total = in_ref[0].astype(F32)
    for g in range(1, GROUP):
        total = total + in_ref[g].astype(F32)
    out_ref[...] = total.astype(BF)


def step_kernel(block_ref, a_ref, b_ref, c_ref, d_ref, accum0_ref, accum1_ref, out_ref):
    total = (a_ref[...].astype(F32) + b_ref[...].astype(F32)) + (c_ref[...].astype(F32) + d_ref[...].astype(F32))
    hot = total[:, PCOL:]
    accum = jnp.concatenate([accum0_ref[...], accum1_ref[...]], axis=1)
    stepped = hot / jnp.sqrt(accum + hot * hot)
    out_ref[...] = jnp.concatenate([total[:, :PCOL], stepped], axis=1).astype(BF)


def spread_kernel(place_ref, own_ref, far_ref, out_ref):
    zp = place_ref[2]
    own, far = own_ref[...], far_ref[...]
    for n in range(NODES):
        out_ref[n, zp] = own
        out_ref[n, 1 - zp] = far


def step(blocks, parts, accum):
    return pl.pallas_call(
        step_kernel,
        out_shape=shape(CHUNK, WIDE),
        grid_spec=pltpu.PrefetchScalarGridSpec(
            num_scalar_prefetch=1,
            grid=(1,),
            in_specs=[VMEM] * ZQ + [
                pl.BlockSpec((CHUNK, E), lambda i, at: (at[0], 0)),
                pl.BlockSpec((CHUNK, E), lambda i, at: (at[1], 0)),
            ],
            out_specs=VMEM,
        ),
        compiler_params=pltpu.CompilerParams(vmem_limit_bytes=16 * MIB),
        cost_estimate=pl.CostEstimate(flops=0, bytes_accessed=2 * MIB, transcendentals=0),
    )(blocks, *parts, accum, accum)


def cold_dense_kernel(place_ref, in_ref, *out_refs):
    node, zq, zp = place_ref[0], place_ref[1], place_ref[2]
    mine = lax.broadcasted_iota(jnp.int32, (NODES, E), 0) == node
    labels = []
    for g in range(GROUP):
        named = jnp.where(mine, in_ref[g, ZQ].astype(F32), 0.0)
        labels.append(jnp.sum(named, axis=0, keepdims=True))
    labels = jnp.concatenate(labels, axis=0).astype(BF)
    entries = GROUP * PAIR
    lane = lax.broadcasted_iota(jnp.int32, (E, entries), 0)
    place = lax.broadcasted_iota(jnp.int32, (E, entries), 1)
    wanted = ((place >> 3) & 1) * NODE_SLOTS + zp * (ZQ * CAP) + (place & 7)
    keep = lax.broadcasted_iota(jnp.int32, (GROUP, entries), 0) == lax.broadcasted_iota(jnp.int32, (GROUP, entries), 1) >> 4
    rows = lax.broadcasted_iota(jnp.int32, (TABLES * COLD_DEV, entries), 0).astype(F32)
    for d, out_ref in enumerate(out_refs):
        target = zq ^ d
        moved = dot(labels, jnp.where(lane == wanted + target * CAP, 1.0, 0.0).astype(BF))
        named = jnp.sum(jnp.where(keep, moved, 0.0), axis=0, keepdims=True)
        onehot = jnp.where(named == rows, 1.0, 0.0).astype(BF)
        out_ref[...] = dot(onehot, in_ref[:, target].reshape(entries, E)).astype(BF)


def cold_step_kernel(accum_ref, a_ref, b_ref, c_ref, d_ref, out_ref):
    total = (a_ref[...].astype(F32) + b_ref[...].astype(F32)) + (c_ref[...].astype(F32) + d_ref[...].astype(F32))
    out_ref[...] = total / jnp.sqrt(accum_ref[...] + total * total)


def finish_kernel(core_ref, in_ref, *refs):
    w1_ref, hot_ref = refs[-2:]
    for n in range(NODES):
        rows = slice(n * CHUNK, (n + 1) * CHUNK)
        for part in range(ZP):
            piece = in_ref[NODES - 1 - n, part]
            w1_ref[rows, part * PCOL:(part + 1) * PCOL] = piece[:, :PCOL]
            for b in range(2):
                at = (2 * part + b) * HALF + n * CHUNK
                hot_ref[at:at + CHUNK, :] = piece[:, PCOL + b * E:PCOL + (b + 1) * E].astype(F32)


def finish(side, half, held=()):
    return pl.pallas_call(
        finish_kernel,
        out_shape=(shape(FEAT, HID), shape(TABLES * HOT, E, dtype=F32)),
        grid_spec=pltpu.PrefetchScalarGridSpec(
            num_scalar_prefetch=1,
            grid=(1,),
            in_specs=[VMEM] + [pl.BlockSpec(memory_space=pl.ANY)] * len(held),
            out_specs=(
                pl.BlockSpec((HALF, HID), lambda i, at: (at[0], 0)),
                pl.BlockSpec((HOT_HALF, E), lambda i, at: (at[0], 0)),
            ),
        ),
        input_output_aliases={2: 0, 3: 1} if held else {},
        compiler_params=pltpu.CompilerParams(vmem_limit_bytes=16 * MIB),
        cost_estimate=pl.CostEstimate(flops=0, bytes_accessed=4 * MIB, transcendentals=0),
    )(side, half, *held)


def on_device(pooled, lookups, converted, w_hidden, w_out, hot_accum, cold_accum):
    me = lax.axis_index("all")
    node, zq, zp, core = me >> 4, (me >> 2) & 3, (me >> 1) & 1, me & 1
    ids = lookups.T
    core_arg = core.reshape(1)
    place = jnp.stack([node, zq, zp])

    def in_hbm(array):
        return pltpu.with_memory_space_constraint(array, pltpu.HBM)

    def flip(array, mask):
        return lax.ppermute(array, "all", [(i, i ^ mask) for i in range(OWNERS)])

    def exchange(array, groups):
        return lax.all_to_all(array, "all", 0, 0, axis_index_groups=groups, tiled=True)

    with_pair = [
        [n * LOCALS + q * 4 + p * 2 + c for n in range(NODES) for p in range(ZP)] for q in range(ZQ) for c in range(2)
    ]
    alone = [
        [n * LOCALS + low for n in reversed(range(NODES))] for low in range(LOCALS)
    ]
    halves = shape(NODES, ZP, CHUNK, WIDE)
    half_w1, half_hot = (NODES, ZP, CHUNK, PCOL), (NODES, ZP, CHUNK, 2 * E)
    w1_send, w1_own, pre, weights, hits = call(
        backprop_kernel,
        (
            pltpu.HBM(half_w1, BF),
            pltpu.VMEM(half_w1, BF),
            pltpu.VMEM((TOK, HID), BF),
            pltpu.VMEM((FEAT, HID), BF),
            pltpu.VMEM((TABLES, HOT, TOK), BF),
        ),
        (core_arg, *map(in_hbm, (pooled, ids, converted.reshape(1, TOK), w_hidden, w_out.reshape(HID // E, E)))),
        scalars=1,
        scratch=[
            pltpu.VMEM((TOK, HID), F32),
            pltpu.VMEM((FEAT, TOK), BF),
            pltpu.VMEM((TOK, FEAT), BF),
            pltpu.VMEM((TABLES, TOK), jnp.int32),
            pltpu.VMEM((1, TOK), jnp.int32),
            pltpu.VMEM((HID // E, E), BF),
            pltpu.VMEM(half_w1, BF),
            pltpu.SemaphoreType.DMA((HID // 256 + 4,)),
            pltpu.SemaphoreType.DMA((ZP,)),
        ],
        spec=HBM,
        out_specs=(HBM, VMEM, VMEM, VMEM, VMEM),
        limit=24,
        flops=3 * 10**9,
        size=8 * MIB,
    )
    w1_far = flip(w1_send, 1)
    hot_send, hot_own, grads = call(
        hot_kernel,
        (pltpu.VMEM(half_hot, BF), pltpu.VMEM(half_hot, BF), shape(TOK, FEAT)),
        (core_arg, pre, weights, hits),
        scalars=1,
        flops=2 * 10**9,
        size=6 * MIB,
    )
    hot_far = flip(hot_send, 1)
    chip = add_part(w1_own, w1_far, 0)
    chip = add_part(hot_own, hot_far, PCOL, chip)
    parts = exchange(chip.reshape(GROUP, CHUNK, WIDE), with_pair)
    cold_send, cold_own = call(
        pack_kernel,
        (shape(SLOT_HALF + NODES, E), shape(SLOT_HALF + NODES, E)),
        (core_arg, ids, grads),
        scalars=1,
        scratch=[pltpu.VMEM((TABLES * TOK, E), BF)],
        flops=6 * 10**9,
        size=8 * MIB,
    )
    slab = call(
        merge_kernel,
        shape(GROUP, SLAB, PAIR, E),
        (core_arg, cold_own, flip(cold_send, 1)),
        scalars=1,
        size=3 * MIB,
    )
    part = call(group_sum_kernel, shape(CHUNK, WIDE), (parts,), size=2 * MIB)
    slab = exchange(slab, with_pair)
    quad = [part] + [flip(part, 4 * d) for d in range(1, ZQ)]
    block = ((core * ZP + zp) * 2 * HALF + node * CHUNK) // CHUNK
    done = step(jnp.stack([block, block + HALF // CHUNK]), quad, hot_accum.reshape(TABLES * HOT, E))
    whole = call(spread_kernel, halves, (place, done, flip(done, 2)), scalars=1, size=2 * MIB)
    half = exchange(whole, alone)
    cold = call(
        cold_dense_kernel,
        tuple(shape(TABLES * COLD_DEV, E) for _ in range(ZQ)),
        (place, slab),
        scalars=1,
        flops=10**9,
        size=2 * MIB,
    )
    cold = [cold[0]] + [flip(cold[d], 4 * d) for d in range(1, ZQ)]
    half, cold = lax.optimization_barrier((half, cold))
    cold_step = call(
        cold_step_kernel,
        shape(TABLES * COLD_DEV, E, dtype=F32),
        (cold_accum.reshape(TABLES * COLD_DEV, E), *cold),
        size=MIB,
    )
    far = flip(half, 1)
    held = finish(core_arg, half)
    w1_grad, hot_step = finish(1 - core_arg, far, held)
    return (w1_grad, hot_step.reshape(TABLES, HOT, E), cold_step.reshape(TABLES, COLD_DEV, E))


def solution(mesh):
    mesh = Mesh(mesh.devices.reshape(OWNERS), ("all",))
    rows = P("all")
    in_specs = (rows, rows, rows, P(), P(), P(), P(None, "all"))
    out_specs = (P(), P(), P(None, "all"))
    return jax.shard_map(on_device, mesh=mesh, in_specs=in_specs, out_specs=out_specs, check_vma=False)
```

```python
import jax
import jax.numpy as jnp
from jax import lax
from jax.experimental import pallas as pl
from jax.experimental.pallas import tpu as pltpu
from jax.sharding import Mesh
from jax.sharding import PartitionSpec as P

CAP = 8
E = 128
HID = 2048
FEAT = 512
TOK = 512
TABLES = 4
HOT = 512
COLD_DEV = 64
NODES = 16
LOCALS = 16
ZQ = 4
ZP = 2
GROUP = NODES * ZP
OWNERS = NODES * LOCALS
HALF = FEAT // 2
CHUNK = HALF // NODES
PCOL = HID // ZP
WIDE = PCOL + 2 * E
HOT_HALF = TABLES * HOT // 2
SLOT_HALF = OWNERS * CAP // 2
NODE_SLOTS = SLOT_HALF // NODES
PAIR = 2 * CAP
SLAB = ZQ + 1
BF = jnp.bfloat16
F32 = jnp.float32
MIB = 1024 * 1024
VMEM = pl.BlockSpec(memory_space=pltpu.VMEM)
HBM = pl.BlockSpec(memory_space=pltpu.HBM)
SMEM = pl.BlockSpec(memory_space=pltpu.SMEM)


def dot(a, b):
    return jnp.dot(a, b, preferred_element_type=F32)


def dot_nt(a, b):
    return lax.dot_general(a, b, (((1,), (1,)), ((), ())), preferred_element_type=F32)


def shape(*dims, dtype=BF):
    return jax.ShapeDtypeStruct(dims, dtype)


def call(kernel, out_shape, args, scalars=0, scratch=(), limit=16, flops=0, size=0, spec=VMEM, out_specs=None):
    many = isinstance(out_shape, (tuple, list))
    return pl.pallas_call(
        kernel,
        out_shape=out_shape,
        in_specs=[SMEM] * scalars + [spec] * (len(args) - scalars),
        out_specs=out_specs or (tuple(VMEM for _ in out_shape) if many else VMEM),
        scratch_shapes=scratch,
        compiler_params=pltpu.CompilerParams(vmem_limit_bytes=limit * MIB),
        cost_estimate=pl.CostEstimate(flops=flops, bytes_accessed=size, transcendentals=0),
    )(*args)


def backprop_kernel(
    core_ref, x_hbm, ids_hbm, y_hbm, wh_hbm, wo_hbm, send_hbm, own_ref, pre_ref, wh_ref, hit_ref,
    slope_ref, xt_ref, x_ref, ids_ref, y_ref, wo_ref, send_ref, sems, out_sems,
):
    core = core_ref[0]
    step = 256
    blocks = HID // step
    loads = [
        pltpu.make_async_copy(wh_hbm.at[:, pl.ds(j * step, step)], wh_ref.at[:, pl.ds(j * step, step)], sems.at[j])
        for j in range(blocks)
    ]
    small = [
        pltpu.make_async_copy(src, dst, sems.at[blocks + i])
        for i, (src, dst) in enumerate(((x_hbm, x_ref), (wo_hbm, wo_ref), (ids_hbm, ids_ref), (y_hbm, y_ref)))
    ]
    stores = []
    for copy in (*small[1:], small[0], *loads):
        copy.start()
    for copy in small[1:]:
        copy.wait()
    hot_iota = lax.broadcasted_iota(jnp.int32, (HOT, TOK), 0)
    for t in range(TABLES):
        hit = ids_ref[t:t + 1, :] == hot_iota
        hit_ref[t] = jnp.where(hit, 1.0, 0.0).astype(BF)
    small[0].wait()
    x = x_ref[...]
    xt_ref[...] = x.T
    wo = wo_ref[...].astype(F32)
    logit = jnp.zeros((TOK, E), F32)
    for j in range(blocks):
        if j % 4 == 0:
            for copy in loads[j:j + 4]:
                copy.wait()
        cols = slice(j * step, (j + 1) * step)
        v = dot(x, wh_ref[:, cols])
        s = jax.nn.sigmoid(v)
        h = v * s
        slope_ref[:, cols] = s + h * (1.0 - s)
        out_row = jnp.concatenate([wo[2 * j:2 * j + 1], wo[2 * j + 1:2 * j + 2]], axis=1)
        out_row = jnp.broadcast_to(out_row, (E, step)).astype(BF)
        logit = logit + dot_nt(h.astype(BF), out_row)
    chance = jax.nn.sigmoid(logit)
    y = jnp.broadcast_to(y_ref[...].astype(F32), (E, TOK)).T
    weight = y * (1.0 + chance) + (1.0 - y) * (1.0 - chance) * (1.0 + chance)
    lg = weight * (chance - y)
    lg = jnp.concatenate([lg] * (step // E), axis=1)
    own_rows = pl.ds(pl.multiple_of(core * HALF, HALF), HALF)
    far_rows = pl.ds(pl.multiple_of((1 - core) * HALF, HALF), HALF)
    for j in range(HID // step):
        cols = slice(j * step, (j + 1) * step)
        out_row = jnp.concatenate([wo[2 * j:2 * j + 1], wo[2 * j + 1:2 * j + 2]], axis=1)
        pre = (lg * out_row * slope_ref[:, cols]).astype(BF)
        pre_ref[:, cols] = pre
        part, at = divmod(j * step, PCOL)
        for rows, out_ref in ((far_rows, send_ref), (own_rows, own_ref)):
            term = dot(xt_ref[rows, :], pre).astype(BF)
            out_ref[:, part, :, at:at + step] = term.reshape(NODES, CHUNK, step)
        if at + step == PCOL:
            copy = pltpu.make_async_copy(send_ref.at[:, part], send_hbm.at[:, part], out_sems.at[part])
            copy.start()
            stores.append(copy)
    for copy in stores:
        copy.wait()


def hot_kernel(core_ref, pre_ref, wh_ref, hit_ref, send_ref, own_ref, grad_ref):
    core = core_ref[0]
    grad_ref[...] = dot_nt(pre_ref[...], wh_ref[...]).astype(BF)
    for side, out_ref in ((1 - core, send_ref), (core, own_ref)):
        for t in range(ZP):
            table = side * 2 + t
            grads = grad_ref[:, pl.ds(pl.multiple_of(table * E, E), E)]
            total = dot(hit_ref[table], grads).astype(BF)
            for b in range(2):
                out_ref[:, t, :, b * E:(b + 1) * E] = total[b * HALF:(b + 1) * HALF].reshape(NODES, CHUNK, E)


def pack_kernel(core_ref, ids_ref, grad_ref, send_ref, own_ref, rows_ref):
    core = core_ref[0]
    owner_iota = lax.broadcasted_iota(jnp.int32, (OWNERS, TOK), 0)
    earlier = lax.broadcasted_iota(jnp.int32, (TOK, TOK), 0) < lax.broadcasted_iota(jnp.int32, (TOK, TOK), 1)
    earlier = jnp.where(earlier, 1.0, 0.0).astype(BF)
    carry = jnp.zeros((OWNERS, 1), F32)
    slots, names = [], []
    for t in range(TABLES):
        ids = ids_ref[t:t + 1, :]
        cold = ids >= HOT
        offset = jnp.where(cold, ids - HOT, 0)
        owner = jnp.where(cold, offset >> 6, -1)
        member = jnp.where(owner == owner_iota, 1.0, 0.0)
        before = dot(member.astype(BF), earlier) + carry
        rank = jnp.sum(member * before, axis=0, keepdims=True).astype(jnp.int32)
        carry = carry + jnp.sum(member, axis=1, keepdims=True)
        core_at, zp_at, zq_at, node_at = owner & 1, (owner >> 1) & 1, (owner >> 2) & 3, owner >> 4
        slot = (((core_at * NODES + node_at) * ZP + zp_at) * ZQ + zq_at) * CAP + rank
        slots.append(jnp.where(cold, slot, -1))
        names.append(((offset & (COLD_DEV - 1)) + t * COLD_DEV).astype(F32))
        rows_ref[t * TOK:(t + 1) * TOK, :] = grad_ref[:, t * E:(t + 1) * E]
    slot_col = jnp.concatenate(slots + slots, axis=0).astype(F32).T.astype(jnp.int32)
    lane = lax.broadcasted_iota(jnp.int32, (TOK, E), 1) - core * NODE_SLOTS
    group = lax.broadcasted_iota(jnp.int32, (NODES, TOK), 0)
    flat = jnp.concatenate(slots, axis=1)
    block = 512
    iota = lax.broadcasted_iota(jnp.int32, (block, TABLES * TOK), 0)
    low = [jnp.where((slot_col[:, t:t + 1] & (NODE_SLOTS - 1)) == lane, 1.0, 0.0).astype(BF) for t in range(TABLES)]
    for side, out_ref in ((1 - core, send_ref), (core, own_ref)):
        labels = jnp.zeros((NODES, E), F32)
        for t in range(TABLES):
            high = jnp.where((slots[t] >> 6) - side * NODES == group, names[t], 0.0).astype(BF)
            labels = labels + dot(high, low[t])
        out_ref[SLOT_HALF:, :] = labels.astype(BF)
        for b in range(SLOT_HALF // block):
            member = jnp.where(flat - (side * SLOT_HALF + b * block) == iota, 1.0, 0.0).astype(BF)
            out_ref[b * block:(b + 1) * block, :] = dot(member, rows_ref[...]).astype(BF)


def add_part(a, b, at, held=None):
    width = a.shape[-1]
    rest = () if held is None else (held,)

    def kernel(a_ref, b_ref, *refs):
        out_hbm, sum_ref, sem = refs[-3:]
        sum_ref[...] = a_ref[...] + b_ref[...]
        copy = pltpu.make_async_copy(sum_ref, out_hbm.at[:, :, :, pl.ds(at, width)], sem)
        copy.start()
        copy.wait()

    return pl.pallas_call(
        kernel,
        out_shape=pltpu.HBM((NODES, ZP, CHUNK, WIDE), BF),
        in_specs=[VMEM] * 2 + [HBM] * len(rest),
        out_specs=HBM,
        scratch_shapes=[pltpu.VMEM(a.shape, BF), pltpu.SemaphoreType.DMA],
        input_output_aliases={2: 0} if rest else {},
        compiler_params=pltpu.CompilerParams(vmem_limit_bytes=8 * MIB),
        cost_estimate=pl.CostEstimate(flops=0, bytes_accessed=2 * MIB, transcendentals=0),
    )(a, b, *rest)


def merge_kernel(core_ref, cold_ref, far_cold_ref, out_ref):
    first = core_ref[0] == 0
    own, far = cold_ref[...].astype(F32), far_cold_ref[...].astype(F32)
    labels = (own[SLOT_HALF:] + far[SLOT_HALF:]).astype(BF)
    own = own[:SLOT_HALF].reshape(GROUP * ZQ, CAP, E)
    far = far[:SLOT_HALF].reshape(GROUP * ZQ, CAP, E)
    pair = [jnp.where(first, own, far), jnp.where(first, far, own)]
    out_ref[:, :ZQ] = jnp.concatenate(pair, axis=1).astype(BF).reshape(GROUP, ZQ, PAIR, E)
    for g in range(GROUP):
        out_ref[g, ZQ] = labels


def group_sum_kernel(in_ref, out_ref):
    total = in_ref[0].astype(F32)
    for g in range(1, GROUP):
        total = total + in_ref[g].astype(F32)
    out_ref[...] = total.astype(BF)


def pick_kernel(at_ref, low_ref, high_ref, out_ref):
    out_ref[:, :E] = low_ref[...]
    out_ref[:, E:] = high_ref[...]


def pick(blocks, accum):
    return pl.pallas_call(
        pick_kernel,
        out_shape=pltpu.VMEM((CHUNK, 2 * E), F32),
        grid_spec=pltpu.PrefetchScalarGridSpec(
            num_scalar_prefetch=1,
            grid=(1,),
            in_specs=[
                pl.BlockSpec((CHUNK, E), lambda i, at: (at[0], 0)),
                pl.BlockSpec((CHUNK, E), lambda i, at: (at[1], 0)),
            ],
            out_specs=VMEM,
        ),
    )(blocks, accum, accum)


def step_kernel(a_ref, b_ref, c_ref, d_ref, accum_ref, out_ref):
    total = (a_ref[...].astype(F32) + b_ref[...].astype(F32)) + (c_ref[...].astype(F32) + d_ref[...].astype(F32))
    hot = total[:, PCOL:]
    out_ref[:, :PCOL] = total[:, :PCOL].astype(BF)
    out_ref[:, PCOL:] = (hot / jnp.sqrt(accum_ref[...] + hot * hot)).astype(BF)


def spread_kernel(part_ref, in_ref, *refs):
    out_hbm, sems = refs[-2:]
    part = part_ref[0]
    copies = [pltpu.make_async_copy(in_ref, out_hbm.at[n, part], sems.at[n]) for n in range(NODES)]
    for copy in copies:
        copy.start()
    for copy in copies:
        copy.wait()


def spread(part, chunk, held=()):
    return pl.pallas_call(
        spread_kernel,
        out_shape=pltpu.HBM((NODES, ZP, CHUNK, WIDE), BF),
        in_specs=[SMEM, VMEM] + [HBM] * len(held),
        out_specs=HBM,
        scratch_shapes=[pltpu.SemaphoreType.DMA((NODES,))],
        input_output_aliases={2: 0} if held else {},
        compiler_params=pltpu.CompilerParams(vmem_limit_bytes=4 * MIB),
        cost_estimate=pl.CostEstimate(flops=0, bytes_accessed=2 * MIB, transcendentals=0),
    )(part, chunk, *held)


def cold_dense_kernel(place_ref, in_ref, *out_refs):
    node, zq, zp = place_ref[0], place_ref[1], place_ref[2]
    mine = lax.broadcasted_iota(jnp.int32, (NODES, E), 0) == node
    labels = []
    for g in range(GROUP):
        named = jnp.where(mine, in_ref[g, ZQ].astype(F32), 0.0)
        labels.append(jnp.sum(named, axis=0, keepdims=True))
    labels = jnp.concatenate(labels, axis=0).astype(BF)
    entries = GROUP * PAIR
    lane = lax.broadcasted_iota(jnp.int32, (E, entries), 0)
    place = lax.broadcasted_iota(jnp.int32, (E, entries), 1)
    wanted = ((place >> 3) & 1) * NODE_SLOTS + zp * (ZQ * CAP) + (place & 7)
    keep = lax.broadcasted_iota(jnp.int32, (GROUP, entries), 0) == lax.broadcasted_iota(jnp.int32, (GROUP, entries), 1) >> 4
    rows = lax.broadcasted_iota(jnp.int32, (TABLES * COLD_DEV, entries), 0).astype(F32)
    for d, out_ref in enumerate(out_refs):
        target = zq ^ d
        moved = dot(labels, jnp.where(lane == wanted + target * CAP, 1.0, 0.0).astype(BF))
        named = jnp.sum(jnp.where(keep, moved, 0.0), axis=0, keepdims=True)
        onehot = jnp.where(named == rows, 1.0, 0.0).astype(BF)
        out_ref[...] = dot(onehot, in_ref[:, target].reshape(entries, E)).astype(BF)


def cold_step_kernel(accum_ref, a_ref, b_ref, c_ref, d_ref, out_ref):
    total = (a_ref[...].astype(F32) + b_ref[...].astype(F32)) + (c_ref[...].astype(F32) + d_ref[...].astype(F32))
    out_ref[...] = total / jnp.sqrt(accum_ref[...] + total * total)


def finish_kernel(core_ref, in_ref, *refs):
    w1_ref, hot_ref = refs[-2:]
    for n in range(NODES):
        rows = slice(n * CHUNK, (n + 1) * CHUNK)
        for part in range(ZP):
            piece = in_ref[NODES - 1 - n, part]
            w1_ref[rows, part * PCOL:(part + 1) * PCOL] = piece[:, :PCOL]
            for b in range(2):
                at = (2 * part + b) * HALF + n * CHUNK
                hot_ref[at:at + CHUNK, :] = piece[:, PCOL + b * E:PCOL + (b + 1) * E].astype(F32)


def finish(side, half, held=()):
    return pl.pallas_call(
        finish_kernel,
        out_shape=(shape(FEAT, HID), shape(TABLES * HOT, E, dtype=F32)),
        grid_spec=pltpu.PrefetchScalarGridSpec(
            num_scalar_prefetch=1,
            grid=(1,),
            in_specs=[VMEM] + [pl.BlockSpec(memory_space=pl.ANY)] * len(held),
            out_specs=(
                pl.BlockSpec((HALF, HID), lambda i, at: (at[0], 0)),
                pl.BlockSpec((HOT_HALF, E), lambda i, at: (at[0], 0)),
            ),
        ),
        input_output_aliases={2: 0, 3: 1} if held else {},
        compiler_params=pltpu.CompilerParams(vmem_limit_bytes=16 * MIB),
        cost_estimate=pl.CostEstimate(flops=0, bytes_accessed=4 * MIB, transcendentals=0),
    )(side, half, *held)


def on_device(pooled, lookups, converted, w_hidden, w_out, hot_accum, cold_accum):
    me = lax.axis_index("all")
    node, zq, zp, core = me >> 4, (me >> 2) & 3, (me >> 1) & 1, me & 1
    ids = lookups.T
    core_arg = core.reshape(1)
    place = jnp.stack([node, zq, zp])

    def in_hbm(array):
        return pltpu.with_memory_space_constraint(array, pltpu.HBM)

    def flip(array, mask):
        return lax.ppermute(array, "all", [(i, i ^ mask) for i in range(OWNERS)])

    def exchange(array, groups):
        return lax.all_to_all(array, "all", 0, 0, axis_index_groups=groups, tiled=True)

    with_pair = [
        [n * LOCALS + q * 4 + p * 2 + c for n in range(NODES) for p in range(ZP)] for q in range(ZQ) for c in range(2)
    ]
    alone = [
        [n * LOCALS + low for n in reversed(range(NODES))] for low in range(LOCALS)
    ]
    halves = shape(NODES, ZP, CHUNK, WIDE)
    half_w1, half_hot = (NODES, ZP, CHUNK, PCOL), (NODES, ZP, CHUNK, 2 * E)
    w1_send, w1_own, pre, weights, hits = call(
        backprop_kernel,
        (
            pltpu.HBM(half_w1, BF),
            pltpu.VMEM(half_w1, BF),
            pltpu.VMEM((TOK, HID), BF),
            pltpu.VMEM((FEAT, HID), BF),
            pltpu.VMEM((TABLES, HOT, TOK), BF),
        ),
        (core_arg, *map(in_hbm, (pooled, ids, converted.reshape(1, TOK), w_hidden, w_out.reshape(HID // E, E)))),
        scalars=1,
        scratch=[
            pltpu.VMEM((TOK, HID), F32),
            pltpu.VMEM((FEAT, TOK), BF),
            pltpu.VMEM((TOK, FEAT), BF),
            pltpu.VMEM((TABLES, TOK), jnp.int32),
            pltpu.VMEM((1, TOK), jnp.int32),
            pltpu.VMEM((HID // E, E), BF),
            pltpu.VMEM(half_w1, BF),
            pltpu.SemaphoreType.DMA((HID // 256 + 4,)),
            pltpu.SemaphoreType.DMA((ZP,)),
        ],
        spec=HBM,
        out_specs=(HBM, VMEM, VMEM, VMEM, VMEM),
        limit=24,
        flops=3 * 10**9,
        size=8 * MIB,
    )
    w1_far = flip(w1_send, 1)
    hot_send, hot_own, grads = call(
        hot_kernel,
        (pltpu.VMEM(half_hot, BF), pltpu.VMEM(half_hot, BF), shape(TOK, FEAT)),
        (core_arg, pre, weights, hits),
        scalars=1,
        flops=2 * 10**9,
        size=6 * MIB,
    )
    hot_far = flip(hot_send, 1)
    chip = add_part(w1_own, w1_far, 0)
    chip = add_part(hot_own, hot_far, PCOL, chip)
    parts = exchange(chip.reshape(GROUP, CHUNK, WIDE), with_pair)
    cold_send, cold_own = call(
        pack_kernel,
        (shape(SLOT_HALF + NODES, E), shape(SLOT_HALF + NODES, E)),
        (core_arg, ids, grads),
        scalars=1,
        scratch=[pltpu.VMEM((TABLES * TOK, E), BF)],
        flops=6 * 10**9,
        size=8 * MIB,
    )
    slab = call(
        merge_kernel,
        shape(GROUP, SLAB, PAIR, E),
        (core_arg, cold_own, flip(cold_send, 1)),
        scalars=1,
        size=3 * MIB,
    )
    block = ((core * ZP + zp) * 2 * HALF + node * CHUNK) // CHUNK
    accum = pick(jnp.stack([block, block + HALF // CHUNK]), in_hbm(hot_accum.reshape(TABLES * HOT, E)))
    slab, accum = lax.optimization_barrier((slab, accum))
    part = call(group_sum_kernel, shape(CHUNK, WIDE), (parts,), size=2 * MIB)
    slab = exchange(slab, with_pair)
    quad = [part] + [flip(part, 4 * d) for d in (2, 1, 3)]
    done = call(step_kernel, pltpu.VMEM((CHUNK, WIDE), BF), (*quad, accum))
    beside = flip(done, 2)
    whole = spread(zp.reshape(1), done)
    whole = spread(1 - zp.reshape(1), beside, (whole,))
    half = exchange(whole, alone)
    cold = call(
        cold_dense_kernel,
        tuple(shape(TABLES * COLD_DEV, E) for _ in range(ZQ)),
        (place, slab),
        scalars=1,
        flops=10**9,
        size=2 * MIB,
    )
    cold = [cold[0]] + [flip(cold[d], 4 * d) for d in (2, 1, 3)]
    half, cold = lax.optimization_barrier((half, cold))
    cold_step = call(
        cold_step_kernel,
        shape(TABLES * COLD_DEV, E, dtype=F32),
        (cold_accum.reshape(TABLES * COLD_DEV, E), *cold),
        size=MIB,
    )
    far = flip(half, 1)
    held = finish(core_arg, half)
    w1_grad, hot_step = finish(1 - core_arg, far, held)
    return (w1_grad, hot_step.reshape(TABLES, HOT, E), cold_step.reshape(TABLES, COLD_DEV, E))


def solution(mesh):
    mesh = Mesh(mesh.devices.reshape(OWNERS), ("all",))
    rows = P("all")
    in_specs = (rows, rows, rows, P(), P(), P(), P(None, "all"))
    out_specs = (P(), P(), P(None, "all"))
    return jax.shard_map(on_device, mesh=mesh, in_specs=in_specs, out_specs=out_specs, check_vma=False)
```

```python
import jax
import jax.numpy as jnp
from jax import lax
from jax.experimental import pallas as pl
from jax.experimental.pallas import tpu as pltpu
from jax.sharding import Mesh
from jax.sharding import PartitionSpec as P

CAP = 8
E = 128
HID = 2048
FEAT = 512
TOK = 512
TABLES = 4
HOT = 512
COLD_DEV = 64
NODES = 16
LOCALS = 16
ZQ = 4
ZP = 2
GROUP = NODES * ZP
OWNERS = NODES * LOCALS
HALF = FEAT // 2
CHUNK = HALF // NODES
PCOL = HID // ZP
WIDE = PCOL + 2 * E
HOT_HALF = TABLES * HOT // 2
SLOT_HALF = OWNERS * CAP // 2
NODE_SLOTS = SLOT_HALF // NODES
PAIR = 2 * CAP
SLAB = ZP * ZQ + 1
BF = jnp.bfloat16
F32 = jnp.float32
MIB = 1024 * 1024
COLD_ORDER = ((0, 2, 1, 3), (0, 3, 2, 1))
VMEM = pl.BlockSpec(memory_space=pltpu.VMEM)
HBM = pl.BlockSpec(memory_space=pltpu.HBM)
SMEM = pl.BlockSpec(memory_space=pltpu.SMEM)


def dot(a, b):
    return jnp.dot(a, b, preferred_element_type=F32)


def dot_nt(a, b):
    return lax.dot_general(a, b, (((1,), (1,)), ((), ())), preferred_element_type=F32)


def shape(*dims, dtype=BF):
    return jax.ShapeDtypeStruct(dims, dtype)


def call(kernel, out_shape, args, scalars=0, scratch=(), limit=16, flops=0, size=0, spec=VMEM, out_specs=None):
    many = isinstance(out_shape, (tuple, list))
    return pl.pallas_call(
        kernel,
        out_shape=out_shape,
        in_specs=[SMEM] * scalars + [spec] * (len(args) - scalars),
        out_specs=out_specs or (tuple(VMEM for _ in out_shape) if many else VMEM),
        scratch_shapes=scratch,
        compiler_params=pltpu.CompilerParams(vmem_limit_bytes=limit * MIB),
        cost_estimate=pl.CostEstimate(flops=flops, bytes_accessed=size, transcendentals=0),
    )(*args)


def backprop_kernel(
    core_ref, x_hbm, ids_hbm, y_hbm, wh_hbm, wo_hbm, send_ref, own_ref, pre_ref, wh_ref, hit_ref,
    slope_ref, xt_ref, x_ref, ids_ref, y_ref, wo_ref, sems,
):
    core = core_ref[0]
    step = 256
    blocks = HID // step
    loads = [
        pltpu.make_async_copy(wh_hbm.at[:, pl.ds(j * step, step)], wh_ref.at[:, pl.ds(j * step, step)], sems.at[j])
        for j in range(blocks)
    ]
    small = [
        pltpu.make_async_copy(src, dst, sems.at[blocks + i])
        for i, (src, dst) in enumerate(((x_hbm, x_ref), (wo_hbm, wo_ref), (ids_hbm, ids_ref), (y_hbm, y_ref)))
    ]
    for copy in (*small[1:], small[0], *loads):
        copy.start()
    for copy in small[1:]:
        copy.wait()
    hot_iota = lax.broadcasted_iota(jnp.int32, (HOT, TOK), 0)
    for t in range(TABLES):
        hit = ids_ref[t:t + 1, :] == hot_iota
        hit_ref[t] = jnp.where(hit, 1.0, 0.0).astype(BF)
    small[0].wait()
    x = x_ref[...]
    xt_ref[...] = x.T
    wo = wo_ref[...].astype(F32)
    logit = jnp.zeros((TOK, E), F32)
    for j in range(blocks):
        if j % 4 == 0:
            for copy in loads[j:j + 4]:
                copy.wait()
        cols = slice(j * step, (j + 1) * step)
        v = dot(x, wh_ref[:, cols])
        s = jax.nn.sigmoid(v)
        h = v * s
        slope_ref[:, cols] = s + h * (1.0 - s)
        out_row = jnp.concatenate([wo[2 * j:2 * j + 1], wo[2 * j + 1:2 * j + 2]], axis=1)
        out_row = jnp.broadcast_to(out_row, (E, step)).astype(BF)
        logit = logit + dot_nt(h.astype(BF), out_row)
    chance = jax.nn.sigmoid(logit)
    y = jnp.broadcast_to(y_ref[...].astype(F32), (E, TOK)).T
    weight = y * (1.0 + chance) + (1.0 - y) * (1.0 - chance) * (1.0 + chance)
    lg = weight * (chance - y)
    lg = jnp.concatenate([lg] * (step // E), axis=1)
    own_rows = pl.ds(pl.multiple_of(core * HALF, HALF), HALF)
    far_rows = pl.ds(pl.multiple_of((1 - core) * HALF, HALF), HALF)
    for j in range(HID // step):
        cols = slice(j * step, (j + 1) * step)
        out_row = jnp.concatenate([wo[2 * j:2 * j + 1], wo[2 * j + 1:2 * j + 2]], axis=1)
        pre = (lg * out_row * slope_ref[:, cols]).astype(BF)
        pre_ref[:, cols] = pre
        part, at = divmod(j * step, PCOL)
        for rows, out_ref in ((far_rows, send_ref), (own_rows, own_ref)):
            term = dot(xt_ref[rows, :], pre).astype(BF)
            out_ref[:, part, :, at:at + step] = term.reshape(NODES, CHUNK, step)


def hot_kernel(core_ref, pre_ref, wh_ref, hit_ref, send_ref, own_ref, grad_ref):
    core = core_ref[0]
    grad_ref[...] = dot_nt(pre_ref[...], wh_ref[...]).astype(BF)
    for side, out_ref in ((1 - core, send_ref), (core, own_ref)):
        for t in range(ZP):
            table = side * 2 + t
            grads = grad_ref[:, pl.ds(pl.multiple_of(table * E, E), E)]
            total = dot(hit_ref[table], grads).astype(BF)
            for b in range(2):
                out_ref[:, t, :, b * E:(b + 1) * E] = total[b * HALF:(b + 1) * HALF].reshape(NODES, CHUNK, E)


def pack_kernel(core_ref, ids_ref, grad_ref, send_ref, own_ref, rows_ref):
    core = core_ref[0]
    owner_iota = lax.broadcasted_iota(jnp.int32, (OWNERS, TOK), 0)
    earlier = lax.broadcasted_iota(jnp.int32, (TOK, TOK), 0) < lax.broadcasted_iota(jnp.int32, (TOK, TOK), 1)
    earlier = jnp.where(earlier, 1.0, 0.0).astype(BF)
    carry = jnp.zeros((OWNERS, 1), F32)
    slots, names = [], []
    for t in range(TABLES):
        ids = ids_ref[t:t + 1, :]
        cold = ids >= HOT
        offset = jnp.where(cold, ids - HOT, 0)
        owner = jnp.where(cold, offset >> 6, -1)
        member = jnp.where(owner == owner_iota, 1.0, 0.0)
        before = dot(member.astype(BF), earlier) + carry
        rank = jnp.sum(member * before, axis=0, keepdims=True).astype(jnp.int32)
        carry = carry + jnp.sum(member, axis=1, keepdims=True)
        turned = ((owner >> 1) + 7) & 7
        core_at, zp_at, zq_at, node_at = owner & 1, turned & 1, turned >> 1, owner >> 4
        slot = (((core_at * NODES + node_at) * ZP + zp_at) * ZQ + zq_at) * CAP + rank
        slots.append(jnp.where(cold, slot, -1))
        names.append(((offset & (COLD_DEV - 1)) + t * COLD_DEV).astype(F32))
        rows_ref[t * TOK:(t + 1) * TOK, :] = grad_ref[:, t * E:(t + 1) * E]
    slot_col = jnp.concatenate(slots + slots, axis=0).astype(F32).T.astype(jnp.int32)
    lane = lax.broadcasted_iota(jnp.int32, (TOK, E), 1) - core * NODE_SLOTS
    group = lax.broadcasted_iota(jnp.int32, (NODES, TOK), 0)
    flat = jnp.concatenate(slots, axis=1)
    block = 512
    iota = lax.broadcasted_iota(jnp.int32, (block, TABLES * TOK), 0)
    low = [jnp.where((slot_col[:, t:t + 1] & (NODE_SLOTS - 1)) == lane, 1.0, 0.0).astype(BF) for t in range(TABLES)]
    for side, out_ref in ((1 - core, send_ref), (core, own_ref)):
        labels = jnp.zeros((NODES, E), F32)
        for t in range(TABLES):
            high = jnp.where((slots[t] >> 6) - side * NODES == group, names[t], 0.0).astype(BF)
            labels = labels + dot(high, low[t])
        out_ref[SLOT_HALF:, :] = labels.astype(BF)
        for b in range(SLOT_HALF // block):
            member = jnp.where(flat - (side * SLOT_HALF + b * block) == iota, 1.0, 0.0).astype(BF)
            out_ref[b * block:(b + 1) * block, :] = dot(member, rows_ref[...]).astype(BF)


def add_part(a, b, at, held=None):
    width = a.shape[-1]
    rest = () if held is None else (held,)

    def kernel(a_ref, b_ref, *refs):
        out_hbm, sum_ref, sem = refs[-3:]
        sum_ref[...] = a_ref[...] + b_ref[...]
        copy = pltpu.make_async_copy(sum_ref, out_hbm.at[:, :, :, pl.ds(at, width)], sem)
        copy.start()
        copy.wait()

    return pl.pallas_call(
        kernel,
        out_shape=pltpu.HBM((NODES, ZP, CHUNK, WIDE), BF),
        in_specs=[VMEM] * 2 + [HBM] * len(rest),
        out_specs=HBM,
        scratch_shapes=[pltpu.VMEM(a.shape, BF), pltpu.SemaphoreType.DMA],
        input_output_aliases={2: 0} if rest else {},
        compiler_params=pltpu.CompilerParams(vmem_limit_bytes=8 * MIB),
        cost_estimate=pl.CostEstimate(flops=0, bytes_accessed=2 * MIB, transcendentals=0),
    )(a, b, *rest)


def cold_split_kernel(place_ref, cold_ref, far_cold_ref, keep_ref, send_ref, rows_ref):
    pair_at, first = place_ref[3], place_ref[4] == 0
    own, far = cold_ref[...].astype(F32), far_cold_ref[...].astype(F32)
    labels = (own[SLOT_HALF:] + far[SLOT_HALF:]).astype(BF)
    own = own[:SLOT_HALF].reshape(GROUP * ZQ, CAP, E)
    far = far[:SLOT_HALF].reshape(GROUP * ZQ, CAP, E)
    pair = [jnp.where(first, own, far), jnp.where(first, far, own)]
    rows_ref[...] = jnp.concatenate(pair, axis=1).astype(BF).reshape(NODES, ZP, ZQ, PAIR, E)
    for side, out_ref in ((pair_at, keep_ref), (1 - pair_at, send_ref)):
        out_ref[:NODES] = rows_ref[:, side]
        out_ref[NODES] = jnp.broadcast_to(labels[None], (ZQ, PAIR, E))


def cold_merge_kernel(place_ref, keep_ref, far_ref, out_ref):
    pair_at = place_ref[3]
    lane = lax.broadcasted_iota(jnp.int32, (NODES, E), 1)
    mine = ((lane >> 5) & 1) == pair_at
    labels = jnp.zeros((NODES, E), F32)
    for side, in_ref in ((pair_at, keep_ref), (1 - pair_at, far_ref)):
        for q in range(ZQ):
            out_ref[:, side * ZQ + q] = in_ref[:NODES, q]
        named = jnp.where(mine, in_ref[NODES, 0].astype(F32), 0.0)
        labels = labels + pltpu.roll(named, ((side - pair_at) * ZQ * CAP) & (E - 1), 1)
    labels = labels.astype(BF)
    for n in range(NODES):
        out_ref[n, SLAB - 1] = labels


def group_sum_kernel(in_ref, out_ref):
    total = in_ref[0].astype(F32)
    for g in range(1, GROUP):
        total = total + in_ref[g].astype(F32)
    out_ref[...] = total.astype(BF)


def pick_kernel(at_ref, low_ref, high_ref, out_ref):
    out_ref[:, :E] = low_ref[...]
    out_ref[:, E:] = high_ref[...]


def pick(blocks, accum):
    return pl.pallas_call(
        pick_kernel,
        out_shape=pltpu.VMEM((CHUNK, 2 * E), F32),
        grid_spec=pltpu.PrefetchScalarGridSpec(
            num_scalar_prefetch=1,
            grid=(1,),
            in_specs=[
                pl.BlockSpec((CHUNK, E), lambda i, at: (at[0], 0)),
                pl.BlockSpec((CHUNK, E), lambda i, at: (at[1], 0)),
            ],
            out_specs=VMEM,
        ),
    )(blocks, accum, accum)


def step_kernel(a_ref, b_ref, c_ref, d_ref, accum_ref, out_ref):
    total = (a_ref[...].astype(F32) + b_ref[...].astype(F32)) + (c_ref[...].astype(F32) + d_ref[...].astype(F32))
    hot = total[:, PCOL:]
    out_ref[:, :PCOL] = total[:, :PCOL].astype(BF)
    out_ref[:, PCOL:] = (hot / jnp.sqrt(accum_ref[...] + hot * hot)).astype(BF)


def spread_kernel(part_ref, in_ref, *refs):
    out_hbm, sems = refs[-2:]
    part = part_ref[0]
    copies = [pltpu.make_async_copy(in_ref, out_hbm.at[n, part], sems.at[n]) for n in range(NODES)]
    for copy in copies:
        copy.start()
    for copy in copies:
        copy.wait()


def spread(part, chunk, held=()):
    return pl.pallas_call(
        spread_kernel,
        out_shape=pltpu.HBM((NODES, ZP, CHUNK, WIDE), BF),
        in_specs=[SMEM, VMEM] + [HBM] * len(held),
        out_specs=HBM,
        scratch_shapes=[pltpu.SemaphoreType.DMA((NODES,))],
        input_output_aliases={2: 0} if held else {},
        compiler_params=pltpu.CompilerParams(vmem_limit_bytes=4 * MIB),
        cost_estimate=pl.CostEstimate(flops=0, bytes_accessed=2 * MIB, transcendentals=0),
    )(part, chunk, *held)


def cold_dense_kernel(place_ref, in_ref, *out_refs):
    core = place_ref[4]
    node, quad_at = place_ref[0], place_ref[2]
    mine = lax.broadcasted_iota(jnp.int32, (NODES, E), 0) == node
    labels = []
    for n in range(NODES):
        named = jnp.where(mine, in_ref[n, SLAB - 1].astype(F32), 0.0)
        labels.append(jnp.sum(named, axis=0, keepdims=True))
    labels = jnp.concatenate(labels, axis=0).astype(BF)
    entries = NODES * PAIR
    lane = lax.broadcasted_iota(jnp.int32, (E, entries), 0)
    place = lax.broadcasted_iota(jnp.int32, (E, entries), 1)
    wanted = ((place >> 3) & 1) * NODE_SLOTS + (place & 7)
    keep = lax.broadcasted_iota(jnp.int32, (NODES, entries), 0) == lax.broadcasted_iota(jnp.int32, (NODES, entries), 1) >> 4
    rows = lax.broadcasted_iota(jnp.int32, (TABLES * COLD_DEV, entries), 0).astype(F32)
    for d, out_ref in enumerate(out_refs):
        d = jnp.where(core == 0, COLD_ORDER[0][d], COLD_ORDER[1][d])
        total = jnp.zeros((TABLES * COLD_DEV, E), F32)
        for side in range(ZP):
            target = side * ZQ + (quad_at ^ d)
            moved = dot(labels, jnp.where(lane == wanted + target * CAP, 1.0, 0.0).astype(BF))
            named = jnp.sum(jnp.where(keep, moved, 0.0), axis=0, keepdims=True)
            onehot = jnp.where(named == rows, 1.0, 0.0).astype(BF)
            total = total + dot(onehot, in_ref[:, target].reshape(entries, E))
        out_ref[...] = total.astype(BF)


def cold_step_kernel(accum_ref, a_ref, b_ref, c_ref, d_ref, out_ref):
    total = (a_ref[...].astype(F32) + b_ref[...].astype(F32)) + (c_ref[...].astype(F32) + d_ref[...].astype(F32))
    out_ref[...] = total / jnp.sqrt(accum_ref[...] + total * total)


def finish_kernel(core_ref, in_ref, *refs):
    w1_ref, hot_ref = refs[-2:]
    for n in range(NODES):
        rows = slice(n * CHUNK, (n + 1) * CHUNK)
        for part in range(ZP):
            piece = in_ref[NODES - 1 - n, part]
            w1_ref[rows, part * PCOL:(part + 1) * PCOL] = piece[:, :PCOL]
            for b in range(2):
                at = (2 * part + b) * HALF + n * CHUNK
                hot_ref[at:at + CHUNK, :] = piece[:, PCOL + b * E:PCOL + (b + 1) * E].astype(F32)


def finish(side, half, held=()):
    return pl.pallas_call(
        finish_kernel,
        out_shape=(shape(FEAT, HID), shape(TABLES * HOT, E, dtype=F32)),
        grid_spec=pltpu.PrefetchScalarGridSpec(
            num_scalar_prefetch=1,
            grid=(1,),
            in_specs=[VMEM] + [pl.BlockSpec(memory_space=pl.ANY)] * len(held),
            out_specs=(
                pl.BlockSpec((HALF, HID), lambda i, at: (at[0], 0)),
                pl.BlockSpec((HOT_HALF, E), lambda i, at: (at[0], 0)),
            ),
        ),
        input_output_aliases={2: 0, 3: 1} if held else {},
        compiler_params=pltpu.CompilerParams(vmem_limit_bytes=16 * MIB),
        cost_estimate=pl.CostEstimate(flops=0, bytes_accessed=4 * MIB, transcendentals=0),
    )(side, half, *held)


def on_device(pooled, lookups, converted, w_hidden, w_out, hot_accum, cold_accum):
    me = lax.axis_index("all")
    node, zq, zp, core = me >> 4, (me >> 2) & 3, (me >> 1) & 1, me & 1
    ids = lookups.T
    core_arg = core.reshape(1)
    turned = ((me >> 1) + 7) & 7
    place = jnp.stack([node, zq, turned >> 1, turned & 1, core])

    def in_hbm(array):
        return pltpu.with_memory_space_constraint(array, pltpu.HBM)

    def flip(array, mask, other=None):
        masks = (mask, mask if other is None else other)
        return lax.ppermute(array, "all", [(i, i ^ masks[i & 1]) for i in range(OWNERS)])

    def exchange(array, groups):
        return lax.all_to_all(array, "all", 0, 0, axis_index_groups=groups, tiled=True)

    def turned_flip(array, mask, other=None):
        masks = (mask, mask if other is None else other)

        def partner(i):
            return (i & ~14) | (((((((i >> 1) + 7) & 7) ^ masks[i & 1]) + 1) & 7) << 1)

        return lax.ppermute(array, "all", [(i, partner(i)) for i in range(OWNERS)])

    with_pair = [
        [n * LOCALS + q * 4 + p * 2 + c for n in range(NODES) for p in range(ZP)] for q in range(ZQ) for c in range(2)
    ]
    by_node = [[n * LOCALS + low for n in range(NODES)] for low in range(LOCALS)]
    alone = [
        [n * LOCALS + low for n in reversed(range(NODES))] for low in range(LOCALS)
    ]
    halves = shape(NODES, ZP, CHUNK, WIDE)
    half_w1, half_hot = (NODES, ZP, CHUNK, PCOL), (NODES, ZP, CHUNK, 2 * E)
    w1_send, w1_own, pre, weights, hits = call(
        backprop_kernel,
        (
            pltpu.VMEM(half_w1, BF),
            pltpu.VMEM(half_w1, BF),
            pltpu.VMEM((TOK, HID), BF),
            pltpu.VMEM((FEAT, HID), BF),
            pltpu.VMEM((TABLES, HOT, TOK), BF),
        ),
        (core_arg, *map(in_hbm, (pooled, ids, converted.reshape(1, TOK), w_hidden, w_out.reshape(HID // E, E)))),
        scalars=1,
        scratch=[
            pltpu.VMEM((TOK, HID), F32),
            pltpu.VMEM((FEAT, TOK), BF),
            pltpu.VMEM((TOK, FEAT), BF),
            pltpu.VMEM((TABLES, TOK), jnp.int32),
            pltpu.VMEM((1, TOK), jnp.int32),
            pltpu.VMEM((HID // E, E), BF),
            pltpu.SemaphoreType.DMA((HID // 256 + 4,)),
        ],
        spec=HBM,
        out_specs=(VMEM,) * 5,
        limit=24,
        flops=3 * 10**9,
        size=8 * MIB,
    )
    w1_far = flip(w1_send, 1)
    hot_send, hot_own, grads = call(
        hot_kernel,
        (pltpu.VMEM(half_hot, BF), pltpu.VMEM(half_hot, BF), shape(TOK, FEAT)),
        (core_arg, pre, weights, hits),
        scalars=1,
        flops=2 * 10**9,
        size=6 * MIB,
    )
    hot_far = flip(hot_send, 1)
    chip = add_part(w1_own, w1_far, 0)
    chip = add_part(hot_own, hot_far, PCOL, chip)
    parts = exchange(chip.reshape(GROUP, CHUNK, WIDE), with_pair)
    cold_send, cold_own = call(
        pack_kernel,
        (shape(SLOT_HALF + NODES, E), shape(SLOT_HALF + NODES, E)),
        (core_arg, ids, grads),
        scalars=1,
        scratch=[pltpu.VMEM((TABLES * TOK, E), BF)],
        flops=6 * 10**9,
        size=8 * MIB,
    )
    cold_keep, cold_give = call(
        cold_split_kernel,
        (shape(NODES + 1, ZQ, PAIR, E), shape(NODES + 1, ZQ, PAIR, E)),
        (place, cold_own, flip(cold_send, 1)),
        scalars=1,
        scratch=[pltpu.VMEM((NODES, ZP, ZQ, PAIR, E), BF)],
        size=2 * MIB,
    )
    slab = call(
        cold_merge_kernel,
        shape(NODES, SLAB, PAIR, E),
        (place, cold_keep, turned_flip(cold_give, 1)),
        scalars=1,
        size=2 * MIB,
    )
    block = ((core * ZP + zp) * 2 * HALF + node * CHUNK) // CHUNK
    accum = pick(jnp.stack([block, block + HALF // CHUNK]), in_hbm(hot_accum.reshape(TABLES * HOT, E)))
    slab, accum = lax.optimization_barrier((slab, accum))
    part = call(group_sum_kernel, shape(CHUNK, WIDE), (parts,), size=2 * MIB)
    slab = exchange(slab, by_node)
    quad = [part] + [flip(part, 4 * d, 4 * e) for d, e in zip((2, 1, 3), (3, 2, 1))]
    done = call(step_kernel, pltpu.VMEM((CHUNK, WIDE), BF), (*quad, accum))
    beside = flip(done, 2)
    whole = spread(zp.reshape(1), done)
    whole = spread(1 - zp.reshape(1), beside, (whole,))
    half = exchange(whole, alone)
    cold = call(
        cold_dense_kernel,
        tuple(shape(TABLES * COLD_DEV, E) for _ in range(ZQ)),
        (place, slab),
        scalars=1,
        flops=10**9,
        size=2 * MIB,
    )
    cold = [cold[0]] + [
        turned_flip(cold[k], 2 * COLD_ORDER[0][k], 2 * COLD_ORDER[1][k]) for k in range(1, ZQ)
    ]
    half, cold = lax.optimization_barrier((half, cold))
    cold_step = call(
        cold_step_kernel,
        shape(TABLES * COLD_DEV, E, dtype=F32),
        (cold_accum.reshape(TABLES * COLD_DEV, E), *cold),
        size=MIB,
    )
    far = flip(half, 1)
    held = finish(core_arg, half)
    w1_grad, hot_step = finish(1 - core_arg, far, held)
    return (w1_grad, hot_step.reshape(TABLES, HOT, E), cold_step.reshape(TABLES, COLD_DEV, E))


def solution(mesh):
    mesh = Mesh(mesh.devices.reshape(OWNERS), ("all",))
    rows = P("all")
    in_specs = (rows, rows, rows, P(), P(), P(), P(None, "all"))
    out_specs = (P(), P(), P(None, "all"))
    return jax.shard_map(on_device, mesh=mesh, in_specs=in_specs, out_specs=out_specs, check_vma=False)
```

```python
import jax
import jax.numpy as jnp
from jax import lax
from jax.experimental import pallas as pl
from jax.experimental.pallas import tpu as pltpu
from jax.sharding import Mesh
from jax.sharding import PartitionSpec as P

CAP = 8
E = 128
HID = 2048
FEAT = 512
TOK = 512
TABLES = 4
HOT = 512
COLD_DEV = 64
NODES = 16
LOCALS = 16
ZQ = 4
ZP = 2
GROUP = NODES * ZP
OWNERS = NODES * LOCALS
HALF = FEAT // 2
CHUNK = HALF // NODES
PCOL = HID // ZP
WIDE = PCOL + 2 * E
HOT_HALF = TABLES * HOT // 2
SLOT_HALF = OWNERS * CAP // 2
NODE_SLOTS = SLOT_HALF // NODES
PAIR = 2 * CAP
SLAB = ZP * ZQ + 1
BF = jnp.bfloat16
F32 = jnp.float32
MIB = 1024 * 1024
COLD_ORDER = ((0, 2, 1, 3), (0, 3, 2, 1))
VMEM = pl.BlockSpec(memory_space=pltpu.VMEM)
HBM = pl.BlockSpec(memory_space=pltpu.HBM)
SMEM = pl.BlockSpec(memory_space=pltpu.SMEM)


def dot(a, b):
    return jnp.dot(a, b, preferred_element_type=F32)


def dot_nt(a, b):
    return lax.dot_general(a, b, (((1,), (1,)), ((), ())), preferred_element_type=F32)


def shape(*dims, dtype=BF):
    return jax.ShapeDtypeStruct(dims, dtype)


def call(kernel, out_shape, args, scalars=0, scratch=(), limit=16, flops=0, size=0, spec=VMEM, out_specs=None):
    many = isinstance(out_shape, (tuple, list))
    return pl.pallas_call(
        kernel,
        out_shape=out_shape,
        in_specs=[SMEM] * scalars + [spec] * (len(args) - scalars),
        out_specs=out_specs or (tuple(VMEM for _ in out_shape) if many else VMEM),
        scratch_shapes=scratch,
        compiler_params=pltpu.CompilerParams(vmem_limit_bytes=limit * MIB),
        cost_estimate=pl.CostEstimate(flops=flops, bytes_accessed=size, transcendentals=0),
    )(*args)


def backprop_kernel(
    core_ref, x_hbm, ids_hbm, y_hbm, wh_hbm, wo_hbm, send_ref, own_ref, pre_ref, wh_ref, hit_ref,
    slope_ref, xt_ref, x_ref, ids_ref, y_ref, wo_ref, sems,
):
    core = core_ref[0]
    step = 256
    blocks = HID // step
    loads = [
        pltpu.make_async_copy(wh_hbm.at[:, pl.ds(j * step, step)], wh_ref.at[:, pl.ds(j * step, step)], sems.at[j])
        for j in range(blocks)
    ]
    small = [
        pltpu.make_async_copy(src, dst, sems.at[blocks + i])
        for i, (src, dst) in enumerate(((x_hbm, x_ref), (wo_hbm, wo_ref), (ids_hbm, ids_ref), (y_hbm, y_ref)))
    ]
    for copy in (*small[1:], small[0], *loads):
        copy.start()
    for copy in small[1:]:
        copy.wait()
    hot_iota = lax.broadcasted_iota(jnp.int32, (HOT, TOK), 0)
    for t in range(TABLES):
        hit = ids_ref[t:t + 1, :] == hot_iota
        hit_ref[t] = jnp.where(hit, 1.0, 0.0).astype(BF)
    small[0].wait()
    x = x_ref[...]
    xt_ref[...] = x.T
    wo = wo_ref[...].astype(F32)
    logit = jnp.zeros((TOK, E), F32)
    for j in range(blocks):
        if j % 4 == 0:
            for copy in loads[j:j + 4]:
                copy.wait()
        cols = slice(j * step, (j + 1) * step)
        v = dot(x, wh_ref[:, cols])
        s = jax.nn.sigmoid(v)
        h = v * s
        slope_ref[:, cols] = s + h * (1.0 - s)
        out_row = jnp.concatenate([wo[2 * j:2 * j + 1], wo[2 * j + 1:2 * j + 2]], axis=1)
        out_row = jnp.broadcast_to(out_row, (E, step)).astype(BF)
        logit = logit + dot_nt(h.astype(BF), out_row)
    chance = jax.nn.sigmoid(logit)
    y = jnp.broadcast_to(y_ref[...].astype(F32), (E, TOK)).T
    weight = y * (1.0 + chance) + (1.0 - y) * (1.0 - chance) * (1.0 + chance)
    lg = weight * (chance - y)
    lg = jnp.concatenate([lg] * (step // E), axis=1)
    own_rows = pl.ds(pl.multiple_of(core * HALF, HALF), HALF)
    far_rows = pl.ds(pl.multiple_of((1 - core) * HALF, HALF), HALF)
    for j in range(HID // step):
        cols = slice(j * step, (j + 1) * step)
        out_row = jnp.concatenate([wo[2 * j:2 * j + 1], wo[2 * j + 1:2 * j + 2]], axis=1)
        pre = (lg * out_row * slope_ref[:, cols]).astype(BF)
        pre_ref[:, cols] = pre
        part, at = divmod(j * step, PCOL)
        for rows, out_ref in ((far_rows, send_ref), (own_rows, own_ref)):
            term = dot(xt_ref[rows, :], pre).astype(BF)
            out_ref[:, part, :, at:at + step] = term.reshape(NODES, CHUNK, step)


def hot_kernel(core_ref, pre_ref, wh_ref, hit_ref, send_ref, own_ref, grad_ref):
    core = core_ref[0]
    grad_ref[...] = dot_nt(pre_ref[...], wh_ref[...]).astype(BF)
    for side, out_ref in ((1 - core, send_ref), (core, own_ref)):
        for t in range(ZP):
            table = side * 2 + t
            grads = grad_ref[:, pl.ds(pl.multiple_of(table * E, E), E)]
            total = dot(hit_ref[table], grads).astype(BF)
            for b in range(2):
                out_ref[:, t, :, b * E:(b + 1) * E] = total[b * HALF:(b + 1) * HALF].reshape(NODES, CHUNK, E)


def pack_kernel(core_ref, ids_ref, grad_ref, send_ref, own_ref, rows_ref):
    core = core_ref[0]
    owner_iota = lax.broadcasted_iota(jnp.int32, (OWNERS, TOK), 0)
    earlier = lax.broadcasted_iota(jnp.int32, (TOK, TOK), 0) < lax.broadcasted_iota(jnp.int32, (TOK, TOK), 1)
    earlier = jnp.where(earlier, 1.0, 0.0).astype(BF)
    carry = jnp.zeros((OWNERS, 1), F32)
    slots, names = [], []
    for t in range(TABLES):
        ids = ids_ref[t:t + 1, :]
        cold = ids >= HOT
        offset = jnp.where(cold, ids - HOT, 0)
        owner = jnp.where(cold, offset >> 6, -1)
        member = jnp.where(owner == owner_iota, 1.0, 0.0)
        before = dot(member.astype(BF), earlier) + carry
        rank = jnp.sum(member * before, axis=0, keepdims=True).astype(jnp.int32)
        carry = carry + jnp.sum(member, axis=1, keepdims=True)
        turned = ((owner >> 1) + 7) & 7
        core_at, zp_at, zq_at, node_at = owner & 1, turned & 1, turned >> 1, owner >> 4
        slot = (((core_at * NODES + node_at) * ZP + zp_at) * ZQ + zq_at) * CAP + rank
        slots.append(jnp.where(cold, slot, -1))
        names.append(((offset & (COLD_DEV - 1)) + t * COLD_DEV).astype(F32))
        rows_ref[t * TOK:(t + 1) * TOK, :] = grad_ref[:, t * E:(t + 1) * E]
    slot_col = jnp.concatenate(slots + slots, axis=0).astype(F32).T.astype(jnp.int32)
    lane = lax.broadcasted_iota(jnp.int32, (TOK, E), 1) - core * NODE_SLOTS
    group = lax.broadcasted_iota(jnp.int32, (NODES, TOK), 0)
    flat = jnp.concatenate(slots, axis=1)
    block = 512
    iota = lax.broadcasted_iota(jnp.int32, (block, TABLES * TOK), 0)
    low = [jnp.where((slot_col[:, t:t + 1] & (NODE_SLOTS - 1)) == lane, 1.0, 0.0).astype(BF) for t in range(TABLES)]
    for side, out_ref in ((1 - core, send_ref), (core, own_ref)):
        labels = jnp.zeros((NODES, E), F32)
        for t in range(TABLES):
            high = jnp.where((slots[t] >> 6) - side * NODES == group, names[t], 0.0).astype(BF)
            labels = labels + dot(high, low[t])
        out_ref[SLOT_HALF:, :] = labels.astype(BF)
        for b in range(SLOT_HALF // block):
            member = jnp.where(flat - (side * SLOT_HALF + b * block) == iota, 1.0, 0.0).astype(BF)
            out_ref[b * block:(b + 1) * block, :] = dot(member, rows_ref[...]).astype(BF)


def add_part(a, b, at, held=None):
    width = a.shape[-1]
    rest = () if held is None else (held,)

    def kernel(a_ref, b_ref, *refs):
        out_hbm, sum_ref, sems = refs[-3:]
        step = NODES // 4
        copies = []
        for j in range(4):
            rows = pl.ds(j * step, step)
            sum_ref[rows] = a_ref[rows] + b_ref[rows]
            copies.append(pltpu.make_async_copy(sum_ref.at[rows], out_hbm.at[rows, :, :, pl.ds(at, width)], sems.at[j]))
            copies[-1].start()
        for copy in copies:
            copy.wait()

    return pl.pallas_call(
        kernel,
        out_shape=pltpu.HBM((NODES, ZP, CHUNK, WIDE), BF),
        in_specs=[VMEM] * 2 + [HBM] * len(rest),
        out_specs=HBM,
        scratch_shapes=[pltpu.VMEM(a.shape, BF), pltpu.SemaphoreType.DMA((4,))],
        input_output_aliases={2: 0} if rest else {},
        compiler_params=pltpu.CompilerParams(vmem_limit_bytes=8 * MIB),
        cost_estimate=pl.CostEstimate(flops=0, bytes_accessed=2 * MIB, transcendentals=0),
    )(a, b, *rest)


def cold_split_kernel(place_ref, cold_ref, far_cold_ref, keep_ref, send_ref, rows_ref):
    pair_at, first = place_ref[3], place_ref[4] == 0
    own, far = cold_ref[...].astype(F32), far_cold_ref[...].astype(F32)
    labels = (own[SLOT_HALF:] + far[SLOT_HALF:]).astype(BF)
    own = own[:SLOT_HALF].reshape(GROUP * ZQ, CAP, E)
    far = far[:SLOT_HALF].reshape(GROUP * ZQ, CAP, E)
    pair = [jnp.where(first, own, far), jnp.where(first, far, own)]
    rows_ref[...] = jnp.concatenate(pair, axis=1).astype(BF).reshape(NODES, ZP, ZQ, PAIR, E)
    for side, out_ref in ((pair_at, keep_ref), (1 - pair_at, send_ref)):
        out_ref[:NODES] = rows_ref[:, side]
        out_ref[NODES] = jnp.broadcast_to(labels[None], (ZQ, PAIR, E))


def cold_merge_kernel(place_ref, keep_ref, far_ref, out_ref):
    pair_at = place_ref[3]
    lane = lax.broadcasted_iota(jnp.int32, (NODES, E), 1)
    mine = ((lane >> 5) & 1) == pair_at
    labels = jnp.zeros((NODES, E), F32)
    for side, in_ref in ((pair_at, keep_ref), (1 - pair_at, far_ref)):
        for q in range(ZQ):
            out_ref[:, side * ZQ + q] = in_ref[:NODES, q]
        named = jnp.where(mine, in_ref[NODES, 0].astype(F32), 0.0)
        labels = labels + pltpu.roll(named, ((side - pair_at) * ZQ * CAP) & (E - 1), 1)
    labels = labels.astype(BF)
    for n in range(NODES):
        out_ref[n, SLAB - 1] = labels


def group_sum_kernel(in_ref, out_ref):
    total = in_ref[0].astype(F32)
    for g in range(1, GROUP):
        total = total + in_ref[g].astype(F32)
    out_ref[...] = total.astype(BF)


def pick_kernel(at_ref, low_ref, high_ref, out_ref):
    out_ref[:, :E] = low_ref[...]
    out_ref[:, E:] = high_ref[...]


def pick(blocks, accum):
    return pl.pallas_call(
        pick_kernel,
        out_shape=pltpu.VMEM((CHUNK, 2 * E), F32),
        grid_spec=pltpu.PrefetchScalarGridSpec(
            num_scalar_prefetch=1,
            grid=(1,),
            in_specs=[
                pl.BlockSpec((CHUNK, E), lambda i, at: (at[0], 0)),
                pl.BlockSpec((CHUNK, E), lambda i, at: (at[1], 0)),
            ],
            out_specs=VMEM,
        ),
    )(blocks, accum, accum)


def step_kernel(a_ref, b_ref, c_ref, d_ref, accum_ref, out_ref):
    total = (a_ref[...].astype(F32) + b_ref[...].astype(F32)) + (c_ref[...].astype(F32) + d_ref[...].astype(F32))
    hot = total[:, PCOL:]
    out_ref[:, :PCOL] = total[:, :PCOL].astype(BF)
    out_ref[:, PCOL:] = (hot / jnp.sqrt(accum_ref[...] + hot * hot)).astype(BF)


def spread_kernel(part_ref, in_ref, *refs):
    out_hbm, many_ref, sems = refs[-3:]
    half = NODES // 2
    many_ref[...] = jnp.broadcast_to(in_ref[...][None], many_ref.shape)
    copies = [
        pltpu.make_async_copy(many_ref, out_hbm.at[pl.ds(k * half, half), part_ref[0]], sems.at[k]) for k in range(2)
    ]
    for copy in copies:
        copy.start()
    for copy in copies:
        copy.wait()


def spread(part, chunk, held=()):
    return pl.pallas_call(
        spread_kernel,
        out_shape=pltpu.HBM((NODES, ZP, CHUNK, WIDE), BF),
        in_specs=[SMEM, VMEM] + [HBM] * len(held),
        out_specs=HBM,
        scratch_shapes=[pltpu.VMEM((NODES // 2, CHUNK, WIDE), BF), pltpu.SemaphoreType.DMA((2,))],
        input_output_aliases={2: 0} if held else {},
        compiler_params=pltpu.CompilerParams(vmem_limit_bytes=4 * MIB),
        cost_estimate=pl.CostEstimate(flops=0, bytes_accessed=2 * MIB, transcendentals=0),
    )(part, chunk, *held)


def cold_dense_kernel(place_ref, in_ref, *out_refs):
    core = place_ref[4]
    node, quad_at = place_ref[0], place_ref[2]
    mine = lax.broadcasted_iota(jnp.int32, (NODES, E), 0) == node
    labels = []
    for n in range(NODES):
        named = jnp.where(mine, in_ref[n, SLAB - 1].astype(F32), 0.0)
        labels.append(jnp.sum(named, axis=0, keepdims=True))
    labels = jnp.concatenate(labels, axis=0).astype(BF)
    entries = NODES * PAIR
    lane = lax.broadcasted_iota(jnp.int32, (E, entries), 0)
    place = lax.broadcasted_iota(jnp.int32, (E, entries), 1)
    wanted = ((place >> 3) & 1) * NODE_SLOTS + (place & 7)
    keep = lax.broadcasted_iota(jnp.int32, (NODES, entries), 0) == lax.broadcasted_iota(jnp.int32, (NODES, entries), 1) >> 4
    rows = lax.broadcasted_iota(jnp.int32, (TABLES * COLD_DEV, entries), 0).astype(F32)
    for d, out_ref in enumerate(out_refs):
        d = jnp.where(core == 0, COLD_ORDER[0][d], COLD_ORDER[1][d])
        total = jnp.zeros((TABLES * COLD_DEV, E), F32)
        for side in range(ZP):
            target = side * ZQ + (quad_at ^ d)
            moved = dot(labels, jnp.where(lane == wanted + target * CAP, 1.0, 0.0).astype(BF))
            named = jnp.sum(jnp.where(keep, moved, 0.0), axis=0, keepdims=True)
            onehot = jnp.where(named == rows, 1.0, 0.0).astype(BF)
            total = total + dot(onehot, in_ref[:, target].reshape(entries, E))
        out_ref[...] = total.astype(BF)


def cold_step_kernel(accum_ref, a_ref, b_ref, c_ref, d_ref, out_ref):
    total = (a_ref[...].astype(F32) + b_ref[...].astype(F32)) + (c_ref[...].astype(F32) + d_ref[...].astype(F32))
    out_ref[...] = total / jnp.sqrt(accum_ref[...] + total * total)


def finish_kernel(core_ref, in_ref, *refs):
    w1_ref, hot_ref = refs[-2:]
    for n in range(NODES):
        rows = slice(n * CHUNK, (n + 1) * CHUNK)
        for part in range(ZP):
            piece = in_ref[NODES - 1 - n, part]
            w1_ref[rows, part * PCOL:(part + 1) * PCOL] = piece[:, :PCOL]
            for b in range(2):
                at = (2 * part + b) * HALF + n * CHUNK
                hot_ref[at:at + CHUNK, :] = piece[:, PCOL + b * E:PCOL + (b + 1) * E].astype(F32)


def finish(side, half, held=()):
    return pl.pallas_call(
        finish_kernel,
        out_shape=(shape(FEAT, HID), shape(TABLES * HOT, E, dtype=F32)),
        grid_spec=pltpu.PrefetchScalarGridSpec(
            num_scalar_prefetch=1,
            grid=(1,),
            in_specs=[VMEM] + [pl.BlockSpec(memory_space=pl.ANY)] * len(held),
            out_specs=(
                pl.BlockSpec((HALF, HID), lambda i, at: (at[0], 0)),
                pl.BlockSpec((HOT_HALF, E), lambda i, at: (at[0], 0)),
            ),
        ),
        input_output_aliases={2: 0, 3: 1} if held else {},
        compiler_params=pltpu.CompilerParams(vmem_limit_bytes=16 * MIB),
        cost_estimate=pl.CostEstimate(flops=0, bytes_accessed=4 * MIB, transcendentals=0),
    )(side, half, *held)


def on_device(pooled, lookups, converted, w_hidden, w_out, hot_accum, cold_accum):
    me = lax.axis_index("all")
    node, zq, zp, core = me >> 4, (me >> 2) & 3, (me >> 1) & 1, me & 1
    ids = lookups.T
    core_arg = core.reshape(1)
    turned = ((me >> 1) + 7) & 7
    place = jnp.stack([node, zq, turned >> 1, turned & 1, core])

    def in_hbm(array):
        return pltpu.with_memory_space_constraint(array, pltpu.HBM)

    def flip(array, mask, other=None):
        masks = (mask, mask if other is None else other)
        return lax.ppermute(array, "all", [(i, i ^ masks[i & 1]) for i in range(OWNERS)])

    def exchange(array, groups):
        return lax.all_to_all(array, "all", 0, 0, axis_index_groups=groups, tiled=True)

    def turned_flip(array, mask, other=None):
        masks = (mask, mask if other is None else other)

        def partner(i):
            return (i & ~14) | (((((((i >> 1) + 7) & 7) ^ masks[i & 1]) + 1) & 7) << 1)

        return lax.ppermute(array, "all", [(i, partner(i)) for i in range(OWNERS)])

    with_pair = [
        [n * LOCALS + q * 4 + p * 2 + c for n in range(NODES) for p in range(ZP)] for q in range(ZQ) for c in range(2)
    ]
    by_node = [[n * LOCALS + low for n in range(NODES)] for low in range(LOCALS)]
    alone = [
        [n * LOCALS + low for n in reversed(range(NODES))] for low in range(LOCALS)
    ]
    halves = shape(NODES, ZP, CHUNK, WIDE)
    half_w1, half_hot = (NODES, ZP, CHUNK, PCOL), (NODES, ZP, CHUNK, 2 * E)
    w1_send, w1_own, pre, weights, hits = call(
        backprop_kernel,
        (
            pltpu.VMEM(half_w1, BF),
            pltpu.VMEM(half_w1, BF),
            pltpu.VMEM((TOK, HID), BF),
            pltpu.VMEM((FEAT, HID), BF),
            pltpu.VMEM((TABLES, HOT, TOK), BF),
        ),
        (core_arg, *map(in_hbm, (pooled, ids, converted.reshape(1, TOK), w_hidden, w_out.reshape(HID // E, E)))),
        scalars=1,
        scratch=[
            pltpu.VMEM((TOK, HID), F32),
            pltpu.VMEM((FEAT, TOK), BF),
            pltpu.VMEM((TOK, FEAT), BF),
            pltpu.VMEM((TABLES, TOK), jnp.int32),
            pltpu.VMEM((1, TOK), jnp.int32),
            pltpu.VMEM((HID // E, E), BF),
            pltpu.SemaphoreType.DMA((HID // 256 + 4,)),
        ],
        spec=HBM,
        out_specs=(VMEM,) * 5,
        limit=24,
        flops=3 * 10**9,
        size=8 * MIB,
    )
    w1_far = flip(w1_send, 1)
    hot_send, hot_own, grads = call(
        hot_kernel,
        (pltpu.VMEM(half_hot, BF), pltpu.VMEM(half_hot, BF), shape(TOK, FEAT)),
        (core_arg, pre, weights, hits),
        scalars=1,
        flops=2 * 10**9,
        size=6 * MIB,
    )
    hot_far = flip(hot_send, 1)
    chip = add_part(w1_own, w1_far, 0)
    chip = add_part(hot_own, hot_far, PCOL, chip)
    parts = exchange(chip.reshape(GROUP, CHUNK, WIDE), with_pair)
    cold_send, cold_own = call(
        pack_kernel,
        (shape(SLOT_HALF + NODES, E), shape(SLOT_HALF + NODES, E)),
        (core_arg, ids, grads),
        scalars=1,
        scratch=[pltpu.VMEM((TABLES * TOK, E), BF)],
        flops=6 * 10**9,
        size=8 * MIB,
    )
    cold_keep, cold_give = call(
        cold_split_kernel,
        (shape(NODES + 1, ZQ, PAIR, E), shape(NODES + 1, ZQ, PAIR, E)),
        (place, cold_own, flip(cold_send, 1)),
        scalars=1,
        scratch=[pltpu.VMEM((NODES, ZP, ZQ, PAIR, E), BF)],
        size=2 * MIB,
    )
    slab = call(
        cold_merge_kernel,
        shape(NODES, SLAB, PAIR, E),
        (place, cold_keep, turned_flip(cold_give, 1)),
        scalars=1,
        size=2 * MIB,
    )
    block = ((core * ZP + zp) * 2 * HALF + node * CHUNK) // CHUNK
    accum = pick(jnp.stack([block, block + HALF // CHUNK]), in_hbm(hot_accum.reshape(TABLES * HOT, E)))
    slab, accum = lax.optimization_barrier((slab, accum))
    part = call(group_sum_kernel, shape(CHUNK, WIDE), (parts,), size=2 * MIB)
    slab = exchange(slab, by_node)
    quad = [part] + [flip(part, 4 * d, 4 * e) for d, e in zip((2, 1, 3), (2, 3, 1))]
    cold = call(
        cold_dense_kernel,
        tuple(shape(TABLES * COLD_DEV, E) for _ in range(ZQ)),
        (place, slab),
        scalars=1,
        flops=10**9,
        size=2 * MIB,
    )
    quad, cold = lax.optimization_barrier((quad, cold))
    done = call(step_kernel, pltpu.VMEM((CHUNK, WIDE), BF), (*quad, accum))
    beside = flip(done, 2)
    whole = spread(zp.reshape(1), done)
    whole = spread(1 - zp.reshape(1), beside, (whole,))
    half = exchange(whole, alone)
    cold = [cold[0]] + [
        turned_flip(cold[k], 2 * COLD_ORDER[0][k], 2 * COLD_ORDER[1][k]) for k in range(1, ZQ)
    ]
    half, cold = lax.optimization_barrier((half, cold))
    cold_step = call(
        cold_step_kernel,
        shape(TABLES * COLD_DEV, E, dtype=F32),
        (cold_accum.reshape(TABLES * COLD_DEV, E), *cold),
        size=MIB,
    )
    far = flip(half, 1)
    held = finish(core_arg, half)
    w1_grad, hot_step = finish(1 - core_arg, far, held)
    return (w1_grad, hot_step.reshape(TABLES, HOT, E), cold_step.reshape(TABLES, COLD_DEV, E))


def solution(mesh):
    mesh = Mesh(mesh.devices.reshape(OWNERS), ("all",))
    rows = P("all")
    in_specs = (rows, rows, rows, P(), P(), P(), P(None, "all"))
    out_specs = (P(), P(), P(None, "all"))
    return jax.shard_map(on_device, mesh=mesh, in_specs=in_specs, out_specs=out_specs, check_vma=False)
```

```python
import jax
import jax.numpy as jnp
from jax import lax
from jax.experimental import pallas as pl
from jax.experimental.pallas import tpu as pltpu
from jax.sharding import Mesh
from jax.sharding import PartitionSpec as P

CAP = 8
E = 128
HID = 2048
FEAT = 512
TOK = 512
TABLES = 4
HOT = 512
COLD_DEV = 64
NODES = 16
LOCALS = 16
ZQ = 4
ZP = 2
GROUP = NODES * ZP
OWNERS = NODES * LOCALS
HALF = FEAT // 2
CHUNK = HALF // NODES
PCOL = HID // ZP
WIDE = PCOL + 2 * E
HOT_HALF = TABLES * HOT // 2
SLOT_HALF = OWNERS * CAP // 2
NODE_SLOTS = SLOT_HALF // NODES
PAIR = 2 * CAP
SLAB = ZP * ZQ + 1
BF = jnp.bfloat16
F32 = jnp.float32
MIB = 1024 * 1024
COLD_ORDER = ((0, 2, 1, 3), (0, 3, 2, 1))
VMEM = pl.BlockSpec(memory_space=pltpu.VMEM)
HBM = pl.BlockSpec(memory_space=pltpu.HBM)
SMEM = pl.BlockSpec(memory_space=pltpu.SMEM)


def dot(a, b):
    return jnp.dot(a, b, preferred_element_type=F32)


def dot_nt(a, b):
    return lax.dot_general(a, b, (((1,), (1,)), ((), ())), preferred_element_type=F32)


def shape(*dims, dtype=BF):
    return jax.ShapeDtypeStruct(dims, dtype)


def call(kernel, out_shape, args, scalars=0, scratch=(), limit=16, flops=0, size=0, spec=VMEM, out_specs=None):
    many = isinstance(out_shape, (tuple, list))
    return pl.pallas_call(
        kernel,
        out_shape=out_shape,
        in_specs=[SMEM] * scalars + [spec] * (len(args) - scalars),
        out_specs=out_specs or (tuple(VMEM for _ in out_shape) if many else VMEM),
        scratch_shapes=scratch,
        compiler_params=pltpu.CompilerParams(vmem_limit_bytes=limit * MIB),
        cost_estimate=pl.CostEstimate(flops=flops, bytes_accessed=size, transcendentals=0),
    )(*args)


def backprop_kernel(
    core_ref, x_hbm, ids_hbm, y_hbm, wh_hbm, wo_hbm, send_ref, own_ref, pre_ref, wh_ref, hit_ref,
    slope_ref, xt_ref, x_ref, ids_ref, y_ref, wo_ref, sems,
):
    core = core_ref[0]
    step = 256
    blocks = HID // step
    loads = [
        pltpu.make_async_copy(wh_hbm.at[:, pl.ds(j * step, step)], wh_ref.at[:, pl.ds(j * step, step)], sems.at[j])
        for j in range(blocks)
    ]
    small = [
        pltpu.make_async_copy(src, dst, sems.at[blocks + i])
        for i, (src, dst) in enumerate(((x_hbm, x_ref), (wo_hbm, wo_ref), (ids_hbm, ids_ref), (y_hbm, y_ref)))
    ]
    for copy in (*small[1:], small[0], *loads):
        copy.start()
    for copy in small[1:]:
        copy.wait()
    hot_iota = lax.broadcasted_iota(jnp.int32, (HOT, TOK), 0)
    for t in range(TABLES):
        hit = ids_ref[t:t + 1, :] == hot_iota
        hit_ref[t] = jnp.where(hit, 1.0, 0.0).astype(BF)
    small[0].wait()
    x = x_ref[...]
    xt_ref[...] = x.T
    wo = wo_ref[...].astype(F32)
    logit = jnp.zeros((TOK, E), F32)
    for j in range(blocks):
        if j % 4 == 0:
            for copy in loads[j:j + 4]:
                copy.wait()
        cols = slice(j * step, (j + 1) * step)
        v = dot(x, wh_ref[:, cols])
        s = jax.nn.sigmoid(v)
        h = v * s
        slope_ref[:, cols] = s + h * (1.0 - s)
        out_row = jnp.concatenate([wo[2 * j:2 * j + 1], wo[2 * j + 1:2 * j + 2]], axis=1)
        out_row = jnp.broadcast_to(out_row, (E, step)).astype(BF)
        logit = logit + dot_nt(h.astype(BF), out_row)
    chance = jax.nn.sigmoid(logit)
    y = jnp.broadcast_to(y_ref[...].astype(F32), (E, TOK)).T
    weight = y * (1.0 + chance) + (1.0 - y) * (1.0 - chance) * (1.0 + chance)
    lg = weight * (chance - y)
    lg = jnp.concatenate([lg] * (step // E), axis=1)
    own_rows = pl.ds(pl.multiple_of(core * HALF, HALF), HALF)
    far_rows = pl.ds(pl.multiple_of((1 - core) * HALF, HALF), HALF)
    for j in range(HID // step):
        cols = slice(j * step, (j + 1) * step)
        out_row = jnp.concatenate([wo[2 * j:2 * j + 1], wo[2 * j + 1:2 * j + 2]], axis=1)
        pre = (lg * out_row * slope_ref[:, cols]).astype(BF)
        pre_ref[:, cols] = pre
        part, at = divmod(j * step, PCOL)
        for rows, out_ref in ((far_rows, send_ref), (own_rows, own_ref)):
            term = dot(xt_ref[rows, :], pre).astype(BF)
            out_ref[:, part, :, at:at + step] = term.reshape(NODES, CHUNK, step)


def hot_kernel(core_ref, pre_ref, wh_ref, hit_ref, send_ref, own_ref, grad_ref):
    core = core_ref[0]
    grad_ref[...] = dot_nt(pre_ref[...], wh_ref[...]).astype(BF)
    for side, out_ref in ((1 - core, send_ref), (core, own_ref)):
        for t in range(ZP):
            table = side * 2 + t
            grads = grad_ref[:, pl.ds(pl.multiple_of(table * E, E), E)]
            total = dot(hit_ref[table], grads).astype(BF)
            for b in range(2):
                out_ref[:, t, :, b * E:(b + 1) * E] = total[b * HALF:(b + 1) * HALF].reshape(NODES, CHUNK, E)


def pack_kernel(core_ref, ids_ref, grad_ref, send_ref, own_ref, rows_ref):
    core = core_ref[0]
    owner_iota = lax.broadcasted_iota(jnp.int32, (OWNERS, TOK), 0)
    earlier = lax.broadcasted_iota(jnp.int32, (TOK, TOK), 0) < lax.broadcasted_iota(jnp.int32, (TOK, TOK), 1)
    earlier = jnp.where(earlier, 1.0, 0.0).astype(BF)
    carry = jnp.zeros((OWNERS, 1), F32)
    slots, names = [], []
    for t in range(TABLES):
        ids = ids_ref[t:t + 1, :]
        cold = ids >= HOT
        offset = jnp.where(cold, ids - HOT, 0)
        owner = jnp.where(cold, offset >> 6, -1)
        member = jnp.where(owner == owner_iota, 1.0, 0.0)
        before = dot(member.astype(BF), earlier) + carry
        rank = jnp.sum(member * before, axis=0, keepdims=True).astype(jnp.int32)
        carry = carry + jnp.sum(member, axis=1, keepdims=True)
        turned = ((owner >> 1) + 7) & 7
        core_at, zp_at, zq_at, node_at = owner & 1, turned & 1, turned >> 1, owner >> 4
        slot = (((core_at * NODES + node_at) * ZP + zp_at) * ZQ + zq_at) * CAP + rank
        slots.append(jnp.where(cold, slot, -1))
        names.append(((offset & (COLD_DEV - 1)) + t * COLD_DEV).astype(F32))
        rows_ref[t * TOK:(t + 1) * TOK, :] = grad_ref[:, t * E:(t + 1) * E]
    slot_col = jnp.concatenate(slots + slots, axis=0).astype(F32).T.astype(jnp.int32)
    lane = lax.broadcasted_iota(jnp.int32, (TOK, E), 1) - core * NODE_SLOTS
    group = lax.broadcasted_iota(jnp.int32, (NODES, TOK), 0)
    flat = jnp.concatenate(slots, axis=1)
    block = 512
    iota = lax.broadcasted_iota(jnp.int32, (block, TABLES * TOK), 0)
    low = [jnp.where((slot_col[:, t:t + 1] & (NODE_SLOTS - 1)) == lane, 1.0, 0.0).astype(BF) for t in range(TABLES)]
    for side, out_ref in ((1 - core, send_ref), (core, own_ref)):
        labels = jnp.zeros((NODES, E), F32)
        for t in range(TABLES):
            high = jnp.where((slots[t] >> 6) - side * NODES == group, names[t], 0.0).astype(BF)
            labels = labels + dot(high, low[t])
        out_ref[SLOT_HALF:, :] = labels.astype(BF)
        for b in range(SLOT_HALF // block):
            member = jnp.where(flat - (side * SLOT_HALF + b * block) == iota, 1.0, 0.0).astype(BF)
            out_ref[b * block:(b + 1) * block, :] = dot(member, rows_ref[...]).astype(BF)


def add_part(a, b, at, held=None):
    width = a.shape[-1]
    rest = () if held is None else (held,)

    def kernel(a_ref, b_ref, *refs):
        out_hbm, sum_ref, sems = refs[-3:]
        step = NODES // 4
        copies = []
        for j in range(4):
            rows = pl.ds(j * step, step)
            sum_ref[rows] = a_ref[rows] + b_ref[rows]
            copies.append(pltpu.make_async_copy(sum_ref.at[rows], out_hbm.at[rows, :, :, pl.ds(at, width)], sems.at[j]))
            copies[-1].start()
        for copy in copies:
            copy.wait()

    return pl.pallas_call(
        kernel,
        out_shape=pltpu.HBM((NODES, ZP, CHUNK, WIDE), BF),
        in_specs=[VMEM] * 2 + [HBM] * len(rest),
        out_specs=HBM,
        scratch_shapes=[pltpu.VMEM(a.shape, BF), pltpu.SemaphoreType.DMA((4,))],
        input_output_aliases={2: 0} if rest else {},
        compiler_params=pltpu.CompilerParams(vmem_limit_bytes=8 * MIB),
        cost_estimate=pl.CostEstimate(flops=0, bytes_accessed=2 * MIB, transcendentals=0),
    )(a, b, *rest)


def cold_split_kernel(place_ref, cold_ref, far_cold_ref, keep_ref, send_ref, rows_ref):
    pair_at, first = place_ref[3], place_ref[4] == 0
    own, far = cold_ref[...].astype(F32), far_cold_ref[...].astype(F32)
    labels = (own[SLOT_HALF:] + far[SLOT_HALF:]).astype(BF)
    own = own[:SLOT_HALF].reshape(GROUP * ZQ, CAP, E)
    far = far[:SLOT_HALF].reshape(GROUP * ZQ, CAP, E)
    pair = [jnp.where(first, own, far), jnp.where(first, far, own)]
    rows_ref[...] = jnp.concatenate(pair, axis=1).astype(BF).reshape(NODES, ZP, ZQ, PAIR, E)
    for side, out_ref in ((pair_at, keep_ref), (1 - pair_at, send_ref)):
        out_ref[:NODES] = rows_ref[:, side]
        out_ref[NODES] = jnp.broadcast_to(labels[None], (ZQ, PAIR, E))


def cold_merge_kernel(place_ref, keep_ref, far_ref, out_ref):
    pair_at = place_ref[3]
    lane = lax.broadcasted_iota(jnp.int32, (NODES, E), 1)
    mine = ((lane >> 5) & 1) == pair_at
    labels = jnp.zeros((NODES, E), F32)
    for side, in_ref in ((pair_at, keep_ref), (1 - pair_at, far_ref)):
        for q in range(ZQ):
            out_ref[:, side * ZQ + q] = in_ref[:NODES, q]
        named = jnp.where(mine, in_ref[NODES, 0].astype(F32), 0.0)
        labels = labels + pltpu.roll(named, ((side - pair_at) * ZQ * CAP) & (E - 1), 1)
    labels = labels.astype(BF)
    for n in range(NODES):
        out_ref[n, SLAB - 1] = labels


def group_sum_kernel(in_ref, out_ref):
    total = in_ref[0].astype(F32)
    for g in range(1, GROUP):
        total = total + in_ref[g].astype(F32)
    out_ref[...] = total.astype(BF)


def pick_kernel(at_ref, low_ref, high_ref, out_ref):
    out_ref[:, :E] = low_ref[...]
    out_ref[:, E:] = high_ref[...]


def pick(blocks, accum):
    return pl.pallas_call(
        pick_kernel,
        out_shape=pltpu.VMEM((CHUNK, 2 * E), F32),
        grid_spec=pltpu.PrefetchScalarGridSpec(
            num_scalar_prefetch=1,
            grid=(1,),
            in_specs=[
                pl.BlockSpec((CHUNK, E), lambda i, at: (at[0], 0)),
                pl.BlockSpec((CHUNK, E), lambda i, at: (at[1], 0)),
            ],
            out_specs=VMEM,
        ),
    )(blocks, accum, accum)


def step_kernel(a_ref, b_ref, c_ref, d_ref, accum_ref, out_ref):
    total = (a_ref[...].astype(F32) + b_ref[...].astype(F32)) + (c_ref[...].astype(F32) + d_ref[...].astype(F32))
    hot = total[:, PCOL:]
    out_ref[:, :PCOL] = total[:, :PCOL].astype(BF)
    out_ref[:, PCOL:] = (hot / jnp.sqrt(accum_ref[...] + hot * hot)).astype(BF)


def spread_kernel(part_ref, in_ref, *refs):
    out_hbm, many_ref, sems = refs[-3:]
    half = NODES // 2
    many_ref[...] = jnp.broadcast_to(in_ref[...][None], many_ref.shape)
    copies = [
        pltpu.make_async_copy(many_ref, out_hbm.at[pl.ds(k * half, half), part_ref[0]], sems.at[k]) for k in range(2)
    ]
    for copy in copies:
        copy.start()
    for copy in copies:
        copy.wait()


def spread(part, chunk, held=()):
    return pl.pallas_call(
        spread_kernel,
        out_shape=pltpu.HBM((NODES, ZP, CHUNK, WIDE), BF),
        in_specs=[SMEM, VMEM] + [HBM] * len(held),
        out_specs=HBM,
        scratch_shapes=[pltpu.VMEM((NODES // 2, CHUNK, WIDE), BF), pltpu.SemaphoreType.DMA((2,))],
        input_output_aliases={2: 0} if held else {},
        compiler_params=pltpu.CompilerParams(vmem_limit_bytes=4 * MIB),
        cost_estimate=pl.CostEstimate(flops=0, bytes_accessed=2 * MIB, transcendentals=0),
    )(part, chunk, *held)


def cold_dense_kernel(place_ref, in_ref, *out_refs):
    core = place_ref[4]
    node, quad_at = place_ref[0], place_ref[2]
    mine = lax.broadcasted_iota(jnp.int32, (NODES, E), 0) == node
    labels = []
    for n in range(NODES):
        named = jnp.where(mine, in_ref[n, SLAB - 1].astype(F32), 0.0)
        labels.append(jnp.sum(named, axis=0, keepdims=True))
    labels = jnp.concatenate(labels, axis=0).astype(BF)
    entries = NODES * PAIR
    lane = lax.broadcasted_iota(jnp.int32, (E, entries), 0)
    place = lax.broadcasted_iota(jnp.int32, (E, entries), 1)
    wanted = ((place >> 3) & 1) * NODE_SLOTS + (place & 7)
    keep = lax.broadcasted_iota(jnp.int32, (NODES, entries), 0) == lax.broadcasted_iota(jnp.int32, (NODES, entries), 1) >> 4
    rows = lax.broadcasted_iota(jnp.int32, (TABLES * COLD_DEV, entries), 0).astype(F32)
    for d, out_ref in enumerate(out_refs):
        d = jnp.where(core == 0, COLD_ORDER[0][d], COLD_ORDER[1][d])
        total = jnp.zeros((TABLES * COLD_DEV, E), F32)
        for side in range(ZP):
            target = side * ZQ + (quad_at ^ d)
            moved = dot(labels, jnp.where(lane == wanted + target * CAP, 1.0, 0.0).astype(BF))
            named = jnp.sum(jnp.where(keep, moved, 0.0), axis=0, keepdims=True)
            onehot = jnp.where(named == rows, 1.0, 0.0).astype(BF)
            total = total + dot(onehot, in_ref[:, target].reshape(entries, E))
        out_ref[...] = total.astype(BF)


def cold_step_kernel(accum_ref, a_ref, b_ref, c_ref, d_ref, out_ref):
    total = (a_ref[...].astype(F32) + b_ref[...].astype(F32)) + (c_ref[...].astype(F32) + d_ref[...].astype(F32))
    out_ref[...] = total / jnp.sqrt(accum_ref[...] + total * total)


def finish_kernel(core_ref, in_ref, *refs):
    w1_ref, hot_ref = refs[-2:]
    for n in range(NODES):
        rows = slice(n * CHUNK, (n + 1) * CHUNK)
        for part in range(ZP):
            piece = in_ref[n, part]
            w1_ref[rows, part * PCOL:(part + 1) * PCOL] = piece[:, :PCOL]
            for b in range(2):
                at = (2 * part + b) * HALF + n * CHUNK
                hot_ref[at:at + CHUNK, :] = piece[:, PCOL + b * E:PCOL + (b + 1) * E].astype(F32)


def finish(side, half, held=()):
    return pl.pallas_call(
        finish_kernel,
        out_shape=(shape(FEAT, HID), shape(TABLES * HOT, E, dtype=F32)),
        grid_spec=pltpu.PrefetchScalarGridSpec(
            num_scalar_prefetch=1,
            grid=(1,),
            in_specs=[VMEM] + [pl.BlockSpec(memory_space=pl.ANY)] * len(held),
            out_specs=(
                pl.BlockSpec((HALF, HID), lambda i, at: (at[0], 0)),
                pl.BlockSpec((HOT_HALF, E), lambda i, at: (at[0], 0)),
            ),
        ),
        input_output_aliases={2: 0, 3: 1} if held else {},
        compiler_params=pltpu.CompilerParams(vmem_limit_bytes=16 * MIB),
        cost_estimate=pl.CostEstimate(flops=0, bytes_accessed=4 * MIB, transcendentals=0),
    )(side, half, *held)


def on_device(pooled, lookups, converted, w_hidden, w_out, hot_accum, cold_accum):
    me = lax.axis_index("all")
    node, zq, zp, core = me >> 4, (me >> 2) & 3, (me >> 1) & 1, me & 1
    ids = lookups.T
    core_arg = core.reshape(1)
    turned = ((me >> 1) + 7) & 7
    place = jnp.stack([node, zq, turned >> 1, turned & 1, core])

    def in_hbm(array):
        return pltpu.with_memory_space_constraint(array, pltpu.HBM)

    def flip(array, mask, other=None):
        masks = (mask, mask if other is None else other)
        return lax.ppermute(array, "all", [(i, i ^ masks[i & 1]) for i in range(OWNERS)])

    def exchange(array, groups):
        return lax.all_to_all(array, "all", 0, 0, axis_index_groups=groups, tiled=True)

    def turned_flip(array, mask, other=None):
        masks = (mask, mask if other is None else other)

        def partner(i):
            return (i & ~14) | (((((((i >> 1) + 7) & 7) ^ masks[i & 1]) + 1) & 7) << 1)

        return lax.ppermute(array, "all", [(i, partner(i)) for i in range(OWNERS)])

    with_pair = [
        [n * LOCALS + q * 4 + p * 2 + c for n in reversed(range(NODES)) for p in reversed(range(ZP))] for q in range(ZQ) for c in range(2)
    ]
    by_node = [[n * LOCALS + low for n in range(NODES)] for low in range(LOCALS)]
    alone = [
        [n * LOCALS + low for n in reversed(range(NODES))] for low in range(LOCALS)
    ]
    halves = shape(NODES, ZP, CHUNK, WIDE)
    half_w1, half_hot = (NODES, ZP, CHUNK, PCOL), (NODES, ZP, CHUNK, 2 * E)
    w1_send, w1_own, pre, weights, hits = call(
        backprop_kernel,
        (
            pltpu.VMEM(half_w1, BF),
            pltpu.VMEM(half_w1, BF),
            pltpu.VMEM((TOK, HID), BF),
            pltpu.VMEM((FEAT, HID), BF),
            pltpu.VMEM((TABLES, HOT, TOK), BF),
        ),
        (core_arg, *map(in_hbm, (pooled, ids, converted.reshape(1, TOK), w_hidden, w_out.reshape(HID // E, E)))),
        scalars=1,
        scratch=[
            pltpu.VMEM((TOK, HID), F32),
            pltpu.VMEM((FEAT, TOK), BF),
            pltpu.VMEM((TOK, FEAT), BF),
            pltpu.VMEM((TABLES, TOK), jnp.int32),
            pltpu.VMEM((1, TOK), jnp.int32),
            pltpu.VMEM((HID // E, E), BF),
            pltpu.SemaphoreType.DMA((HID // 256 + 4,)),
        ],
        spec=HBM,
        out_specs=(VMEM,) * 5,
        limit=24,
        flops=3 * 10**9,
        size=8 * MIB,
    )
    w1_far = flip(w1_send, 1)
    hot_send, hot_own, grads = call(
        hot_kernel,
        (pltpu.VMEM(half_hot, BF), pltpu.VMEM(half_hot, BF), shape(TOK, FEAT)),
        (core_arg, pre, weights, hits),
        scalars=1,
        flops=2 * 10**9,
        size=6 * MIB,
    )
    hot_far = flip(hot_send, 1)
    chip = add_part(w1_own, w1_far, 0)
    chip = add_part(hot_own, hot_far, PCOL, chip)
    parts = exchange(chip.reshape(GROUP, CHUNK, WIDE), with_pair)
    cold_send, cold_own = call(
        pack_kernel,
        (shape(SLOT_HALF + NODES, E), shape(SLOT_HALF + NODES, E)),
        (core_arg, ids, grads),
        scalars=1,
        scratch=[pltpu.VMEM((TABLES * TOK, E), BF)],
        flops=6 * 10**9,
        size=8 * MIB,
    )
    cold_keep, cold_give = call(
        cold_split_kernel,
        (shape(NODES + 1, ZQ, PAIR, E), shape(NODES + 1, ZQ, PAIR, E)),
        (place, cold_own, flip(cold_send, 1)),
        scalars=1,
        scratch=[pltpu.VMEM((NODES, ZP, ZQ, PAIR, E), BF)],
        size=2 * MIB,
    )
    slab = call(
        cold_merge_kernel,
        shape(NODES, SLAB, PAIR, E),
        (place, cold_keep, turned_flip(cold_give, 1)),
        scalars=1,
        size=2 * MIB,
    )
    block = ((core * ZP + 1 - zp) * 2 * HALF + (NODES - 1 - node) * CHUNK) // CHUNK
    accum = pick(jnp.stack([block, block + HALF // CHUNK]), in_hbm(hot_accum.reshape(TABLES * HOT, E)))
    slab, accum = lax.optimization_barrier((slab, accum))
    part = call(group_sum_kernel, shape(CHUNK, WIDE), (parts,), size=2 * MIB)
    slab = exchange(slab, by_node)
    quad = [part] + [flip(part, 4 * d, 4 * e) for d, e in zip((2, 1, 3), (2, 3, 1))]
    cold = call(
        cold_dense_kernel,
        tuple(shape(TABLES * COLD_DEV, E) for _ in range(ZQ)),
        (place, slab),
        scalars=1,
        flops=10**9,
        size=2 * MIB,
    )
    quad, cold = lax.optimization_barrier((quad, cold))
    done = call(step_kernel, pltpu.VMEM((CHUNK, WIDE), BF), (*quad, accum))
    beside = flip(done, 2)
    whole = spread(1 - zp.reshape(1), done)
    whole = spread(zp.reshape(1), beside, (whole,))
    half = exchange(whole, alone)
    cold = [cold[0]] + [
        turned_flip(cold[k], 2 * COLD_ORDER[0][k], 2 * COLD_ORDER[1][k]) for k in range(1, ZQ)
    ]
    half, cold = lax.optimization_barrier((half, cold))
    cold_step = call(
        cold_step_kernel,
        shape(TABLES * COLD_DEV, E, dtype=F32),
        (cold_accum.reshape(TABLES * COLD_DEV, E), *cold),
        size=MIB,
    )
    far = flip(half, 1)
    held = finish(core_arg, half)
    w1_grad, hot_step = finish(1 - core_arg, far, held)
    return (w1_grad, hot_step.reshape(TABLES, HOT, E), cold_step.reshape(TABLES, COLD_DEV, E))


def solution(mesh):
    mesh = Mesh(mesh.devices.reshape(OWNERS), ("all",))
    rows = P("all")
    in_specs = (rows, rows, rows, P(), P(), P(), P(None, "all"))
    out_specs = (P(), P(), P(None, "all"))
    return jax.shard_map(on_device, mesh=mesh, in_specs=in_specs, out_specs=out_specs, check_vma=False)
```

```python
import jax
import jax.numpy as jnp
from jax import lax
from jax.experimental import pallas as pl
from jax.experimental.pallas import tpu as pltpu
from jax.sharding import Mesh
from jax.sharding import PartitionSpec as P

CAP = 8
E = 128
HID = 2048
FEAT = 512
TOK = 512
TABLES = 4
HOT = 512
COLD_DEV = 64
NODES = 16
LOCALS = 16
ZQ = 4
ZP = 2
GROUP = NODES * ZP
OWNERS = NODES * LOCALS
HALF = FEAT // 2
CHUNK = HALF // NODES
PCOL = HID // ZP
WIDE = PCOL + 2 * E
HOT_HALF = TABLES * HOT // 2
SLOT_HALF = OWNERS * CAP // 2
NODE_SLOTS = SLOT_HALF // NODES
PAIR = 2 * CAP
SLAB = ZP * ZQ + 1
BF = jnp.bfloat16
F32 = jnp.float32
MIB = 1024 * 1024
COLD_ORDER = ((0, 2, 1, 3), (0, 3, 2, 1))
VMEM = pl.BlockSpec(memory_space=pltpu.VMEM)
HBM = pl.BlockSpec(memory_space=pltpu.HBM)
SMEM = pl.BlockSpec(memory_space=pltpu.SMEM)


def dot(a, b):
    return jnp.dot(a, b, preferred_element_type=F32)


def dot_nt(a, b):
    return lax.dot_general(a, b, (((1,), (1,)), ((), ())), preferred_element_type=F32)


def shape(*dims, dtype=BF):
    return jax.ShapeDtypeStruct(dims, dtype)


def call(kernel, out_shape, args, scalars=0, scratch=(), limit=16, flops=0, size=0, spec=VMEM, out_specs=None):
    many = isinstance(out_shape, (tuple, list))
    return pl.pallas_call(
        kernel,
        out_shape=out_shape,
        in_specs=[SMEM] * scalars + [spec] * (len(args) - scalars),
        out_specs=out_specs or (tuple(VMEM for _ in out_shape) if many else VMEM),
        scratch_shapes=scratch,
        compiler_params=pltpu.CompilerParams(vmem_limit_bytes=limit * MIB),
        cost_estimate=pl.CostEstimate(flops=flops, bytes_accessed=size, transcendentals=0),
    )(*args)


def backprop_kernel(
    core_ref, x_hbm, ids_hbm, y_hbm, wh_hbm, wo_hbm, send_ref, own_ref, pre_ref, wh_ref, hit_ref,
    slope_ref, xt_ref, x_ref, ids_ref, y_ref, wo_ref, sems,
):
    core = core_ref[0]
    step = 256
    blocks = HID // step
    loads = [
        pltpu.make_async_copy(wh_hbm.at[:, pl.ds(j * step, step)], wh_ref.at[:, pl.ds(j * step, step)], sems.at[j])
        for j in range(blocks)
    ]
    small = [
        pltpu.make_async_copy(src, dst, sems.at[blocks + i])
        for i, (src, dst) in enumerate(((x_hbm, x_ref), (wo_hbm, wo_ref), (ids_hbm, ids_ref), (y_hbm, y_ref)))
    ]
    for copy in (*small[1:], small[0], *loads):
        copy.start()
    for copy in small[1:]:
        copy.wait()
    hot_iota = lax.broadcasted_iota(jnp.int32, (HOT, TOK), 0)
    for t in range(TABLES):
        hit = ids_ref[t:t + 1, :] == hot_iota
        hit_ref[t] = jnp.where(hit, 1.0, 0.0).astype(BF)
    small[0].wait()
    x = x_ref[...]
    xt_ref[...] = x.T
    wo = wo_ref[...].astype(F32)
    logit = jnp.zeros((TOK, E), F32)
    for j in range(blocks):
        if j % 4 == 0:
            for copy in loads[j:j + 4]:
                copy.wait()
        cols = slice(j * step, (j + 1) * step)
        v = dot(x, wh_ref[:, cols])
        s = jax.nn.sigmoid(v)
        h = v * s
        slope_ref[:, cols] = s + h * (1.0 - s)
        out_row = jnp.concatenate([wo[2 * j:2 * j + 1], wo[2 * j + 1:2 * j + 2]], axis=1)
        out_row = jnp.broadcast_to(out_row, (E, step)).astype(BF)
        logit = logit + dot_nt(h.astype(BF), out_row)
    chance = jax.nn.sigmoid(logit)
    y = jnp.broadcast_to(y_ref[...].astype(F32), (E, TOK)).T
    weight = y * (1.0 + chance) + (1.0 - y) * (1.0 - chance) * (1.0 + chance)
    lg = weight * (chance - y)
    lg = jnp.concatenate([lg] * (step // E), axis=1)
    own_rows = pl.ds(pl.multiple_of(core * HALF, HALF), HALF)
    far_rows = pl.ds(pl.multiple_of((1 - core) * HALF, HALF), HALF)
    for j in range(HID // step):
        cols = slice(j * step, (j + 1) * step)
        out_row = jnp.concatenate([wo[2 * j:2 * j + 1], wo[2 * j + 1:2 * j + 2]], axis=1)
        pre = (lg * out_row * slope_ref[:, cols]).astype(BF)
        pre_ref[:, cols] = pre
        part, at = divmod(j * step, PCOL)
        for rows, out_ref in ((far_rows, send_ref), (own_rows, own_ref)):
            term = dot(xt_ref[rows, :], pre).astype(BF)
            out_ref[:, part, :, at:at + step] = term.reshape(NODES, CHUNK, step)


def hot_kernel(core_ref, pre_ref, wh_ref, hit_ref, send_ref, own_ref, grad_ref):
    core = core_ref[0]
    grad_ref[...] = dot_nt(pre_ref[...], wh_ref[...]).astype(BF)
    for side, out_ref in ((1 - core, send_ref), (core, own_ref)):
        for t in range(ZP):
            table = side * 2 + t
            grads = grad_ref[:, pl.ds(pl.multiple_of(table * E, E), E)]
            total = dot(hit_ref[table], grads).astype(BF)
            for b in range(2):
                out_ref[:, t, :, b * E:(b + 1) * E] = total[b * HALF:(b + 1) * HALF].reshape(NODES, CHUNK, E)


def pack_kernel(core_ref, ids_ref, grad_ref, send_ref, own_ref, rows_ref):
    core = core_ref[0]
    owner_iota = lax.broadcasted_iota(jnp.int32, (OWNERS, TOK), 0)
    earlier = lax.broadcasted_iota(jnp.int32, (TOK, TOK), 0) < lax.broadcasted_iota(jnp.int32, (TOK, TOK), 1)
    earlier = jnp.where(earlier, 1.0, 0.0).astype(BF)
    carry = jnp.zeros((OWNERS, 1), F32)
    slots, names = [], []
    for t in range(TABLES):
        ids = ids_ref[t:t + 1, :]
        cold = ids >= HOT
        offset = jnp.where(cold, ids - HOT, 0)
        owner = jnp.where(cold, offset >> 6, -1)
        member = jnp.where(owner == owner_iota, 1.0, 0.0)
        before = dot(member.astype(BF), earlier) + carry
        rank = jnp.sum(member * before, axis=0, keepdims=True).astype(jnp.int32)
        carry = carry + jnp.sum(member, axis=1, keepdims=True)
        turned = ((owner >> 1) + 7) & 7
        core_at, zp_at, zq_at, node_at = owner & 1, turned & 1, turned >> 1, owner >> 4
        slot = (((core_at * NODES + node_at) * ZP + zp_at) * ZQ + zq_at) * CAP + rank
        slots.append(jnp.where(cold, slot, -1))
        names.append(((offset & (COLD_DEV - 1)) + t * COLD_DEV).astype(F32))
        rows_ref[t * TOK:(t + 1) * TOK, :] = grad_ref[:, t * E:(t + 1) * E]
    slot_col = jnp.concatenate(slots + slots, axis=0).astype(F32).T.astype(jnp.int32)
    lane = lax.broadcasted_iota(jnp.int32, (TOK, E), 1) - core * NODE_SLOTS
    group = lax.broadcasted_iota(jnp.int32, (NODES, TOK), 0)
    flat = jnp.concatenate(slots, axis=1)
    block = 512
    iota = lax.broadcasted_iota(jnp.int32, (block, TABLES * TOK), 0)
    low = [jnp.where((slot_col[:, t:t + 1] & (NODE_SLOTS - 1)) == lane, 1.0, 0.0).astype(BF) for t in range(TABLES)]
    for side, out_ref in ((1 - core, send_ref), (core, own_ref)):
        labels = jnp.zeros((NODES, E), F32)
        for t in range(TABLES):
            high = jnp.where((slots[t] >> 6) - side * NODES == group, names[t], 0.0).astype(BF)
            labels = labels + dot(high, low[t])
        out_ref[SLOT_HALF:, :] = labels.astype(BF)
        for b in range(SLOT_HALF // block):
            member = jnp.where(flat - (side * SLOT_HALF + b * block) == iota, 1.0, 0.0).astype(BF)
            out_ref[b * block:(b + 1) * block, :] = dot(member, rows_ref[...]).astype(BF)


def add_part(a, b, at, held=None):
    width = a.shape[-1]
    rest = () if held is None else (held,)

    def kernel(a_ref, b_ref, *refs):
        out_hbm, sum_ref, sems = refs[-3:]
        step = NODES // 4
        copies = []
        for j in range(4):
            rows = pl.ds(j * step, step)
            sum_ref[rows] = a_ref[rows] + b_ref[rows]
            copies.append(pltpu.make_async_copy(sum_ref.at[rows], out_hbm.at[rows, :, :, pl.ds(at, width)], sems.at[j]))
            copies[-1].start()
        for copy in copies:
            copy.wait()

    return pl.pallas_call(
        kernel,
        out_shape=pltpu.HBM((NODES, ZP, CHUNK, WIDE), BF),
        in_specs=[VMEM] * 2 + [HBM] * len(rest),
        out_specs=HBM,
        scratch_shapes=[pltpu.VMEM(a.shape, BF), pltpu.SemaphoreType.DMA((4,))],
        input_output_aliases={2: 0} if rest else {},
        compiler_params=pltpu.CompilerParams(vmem_limit_bytes=8 * MIB),
        cost_estimate=pl.CostEstimate(flops=0, bytes_accessed=2 * MIB, transcendentals=0),
    )(a, b, *rest)


def cold_split_kernel(place_ref, cold_ref, far_cold_ref, keep_ref, send_ref, rows_ref):
    pair_at, first = place_ref[3], place_ref[4] == 0
    own, far = cold_ref[...].astype(F32), far_cold_ref[...].astype(F32)
    labels = (own[SLOT_HALF:] + far[SLOT_HALF:]).astype(BF)
    own = own[:SLOT_HALF].reshape(GROUP * ZQ, CAP, E)
    far = far[:SLOT_HALF].reshape(GROUP * ZQ, CAP, E)
    pair = [jnp.where(first, own, far), jnp.where(first, far, own)]
    rows_ref[...] = jnp.concatenate(pair, axis=1).astype(BF).reshape(NODES, ZP, ZQ, PAIR, E)
    for side, out_ref in ((pair_at, keep_ref), (1 - pair_at, send_ref)):
        out_ref[:NODES] = rows_ref[:, side]
        out_ref[NODES] = jnp.broadcast_to(labels[None], (ZQ, PAIR, E))


def cold_merge_kernel(place_ref, keep_ref, far_ref, out_ref):
    pair_at = place_ref[3]
    lane = lax.broadcasted_iota(jnp.int32, (NODES, E), 1)
    mine = ((lane >> 5) & 1) == pair_at
    labels = jnp.zeros((NODES, E), F32)
    for side, in_ref in ((pair_at, keep_ref), (1 - pair_at, far_ref)):
        for q in range(ZQ):
            out_ref[:, side * ZQ + q] = in_ref[:NODES, q]
        named = jnp.where(mine, in_ref[NODES, 0].astype(F32), 0.0)
        labels = labels + pltpu.roll(named, ((side - pair_at) * ZQ * CAP) & (E - 1), 1)
    labels = labels.astype(BF)
    for n in range(NODES):
        out_ref[n, SLAB - 1] = labels


def group_sum_kernel(in_ref, out_ref):
    total = in_ref[0].astype(F32)
    for g in range(1, GROUP):
        total = total + in_ref[g].astype(F32)
    out_ref[...] = total.astype(BF)


def pick_kernel(at_ref, low_ref, high_ref, out_ref):
    out_ref[:, :E] = low_ref[...]
    out_ref[:, E:] = high_ref[...]


def pick(blocks, accum):
    return pl.pallas_call(
        pick_kernel,
        out_shape=pltpu.VMEM((CHUNK, 2 * E), F32),
        grid_spec=pltpu.PrefetchScalarGridSpec(
            num_scalar_prefetch=1,
            grid=(1,),
            in_specs=[
                pl.BlockSpec((CHUNK, E), lambda i, at: (at[0], 0)),
                pl.BlockSpec((CHUNK, E), lambda i, at: (at[1], 0)),
            ],
            out_specs=VMEM,
        ),
    )(blocks, accum, accum)


def step_kernel(a_ref, b_ref, c_ref, d_ref, accum_ref, out_ref):
    total = (a_ref[...].astype(F32) + b_ref[...].astype(F32)) + (c_ref[...].astype(F32) + d_ref[...].astype(F32))
    hot = total[:, PCOL:]
    out_ref[:, :PCOL] = total[:, :PCOL].astype(BF)
    out_ref[:, PCOL:] = (hot / jnp.sqrt(accum_ref[...] + hot * hot)).astype(BF)


def spread_kernel(part_ref, in_ref, *refs):
    out_hbm, many_ref, sems = refs[-3:]
    half = NODES // 2
    many_ref[...] = jnp.broadcast_to(in_ref[...][None], many_ref.shape)
    copies = [
        pltpu.make_async_copy(many_ref, out_hbm.at[pl.ds(k * half, half), part_ref[0]], sems.at[k]) for k in range(2)
    ]
    for copy in copies:
        copy.start()
    for copy in copies:
        copy.wait()


def spread(part, chunk, held=()):
    return pl.pallas_call(
        spread_kernel,
        out_shape=pltpu.HBM((NODES, ZP, CHUNK, WIDE), BF),
        in_specs=[SMEM, VMEM] + [HBM] * len(held),
        out_specs=HBM,
        scratch_shapes=[pltpu.VMEM((NODES // 2, CHUNK, WIDE), BF), pltpu.SemaphoreType.DMA((2,))],
        input_output_aliases={2: 0} if held else {},
        compiler_params=pltpu.CompilerParams(vmem_limit_bytes=4 * MIB),
        cost_estimate=pl.CostEstimate(flops=0, bytes_accessed=2 * MIB, transcendentals=0),
    )(part, chunk, *held)


def cold_dense_kernel(place_ref, in_ref, *out_refs):
    core = place_ref[4]
    node, quad_at = place_ref[0], place_ref[2]
    mine = lax.broadcasted_iota(jnp.int32, (NODES, E), 0) == node
    labels = []
    for n in range(NODES):
        named = jnp.where(mine, in_ref[n, SLAB - 1].astype(F32), 0.0)
        labels.append(jnp.sum(named, axis=0, keepdims=True))
    labels = jnp.concatenate(labels, axis=0).astype(BF)
    entries = NODES * PAIR
    lane = lax.broadcasted_iota(jnp.int32, (E, entries), 0)
    place = lax.broadcasted_iota(jnp.int32, (E, entries), 1)
    wanted = ((place >> 3) & 1) * NODE_SLOTS + (place & 7)
    keep = lax.broadcasted_iota(jnp.int32, (NODES, entries), 0) == lax.broadcasted_iota(jnp.int32, (NODES, entries), 1) >> 4
    rows = lax.broadcasted_iota(jnp.int32, (TABLES * COLD_DEV, entries), 0).astype(F32)
    for d, out_ref in enumerate(out_refs):
        d = jnp.where(core == 0, COLD_ORDER[0][d], COLD_ORDER[1][d])
        total = jnp.zeros((TABLES * COLD_DEV, E), F32)
        for side in range(ZP):
            target = side * ZQ + (quad_at ^ d)
            moved = dot(labels, jnp.where(lane == wanted + target * CAP, 1.0, 0.0).astype(BF))
            named = jnp.sum(jnp.where(keep, moved, 0.0), axis=0, keepdims=True)
            onehot = jnp.where(named == rows, 1.0, 0.0).astype(BF)
            total = total + dot(onehot, in_ref[:, target].reshape(entries, E))
        out_ref[...] = total.astype(BF)


def cold_step_kernel(accum_ref, a_ref, b_ref, c_ref, d_ref, out_ref):
    total = (a_ref[...].astype(F32) + b_ref[...].astype(F32)) + (c_ref[...].astype(F32) + d_ref[...].astype(F32))
    out_ref[...] = total / jnp.sqrt(accum_ref[...] + total * total)


def finish_kernel(core_ref, in_ref, *refs):
    w1_ref, hot_ref = refs[-2:]
    for n in range(NODES):
        rows = slice(n * CHUNK, (n + 1) * CHUNK)
        for part in range(ZP):
            piece = in_ref[n, part]
            w1_ref[rows, part * PCOL:(part + 1) * PCOL] = piece[:, :PCOL]
            for b in range(2):
                at = (2 * part + b) * HALF + n * CHUNK
                hot_ref[at:at + CHUNK, :] = piece[:, PCOL + b * E:PCOL + (b + 1) * E].astype(F32)


def finish(side, half, held=()):
    return pl.pallas_call(
        finish_kernel,
        out_shape=(shape(FEAT, HID), shape(TABLES * HOT, E, dtype=F32)),
        grid_spec=pltpu.PrefetchScalarGridSpec(
            num_scalar_prefetch=1,
            grid=(1,),
            in_specs=[VMEM] + [pl.BlockSpec(memory_space=pl.ANY)] * len(held),
            out_specs=(
                pl.BlockSpec((HALF, HID), lambda i, at: (at[0], 0)),
                pl.BlockSpec((HOT_HALF, E), lambda i, at: (at[0], 0)),
            ),
        ),
        input_output_aliases={2: 0, 3: 1} if held else {},
        compiler_params=pltpu.CompilerParams(vmem_limit_bytes=16 * MIB),
        cost_estimate=pl.CostEstimate(flops=0, bytes_accessed=4 * MIB, transcendentals=0),
    )(side, half, *held)


def on_device(pooled, lookups, converted, w_hidden, w_out, hot_accum, cold_accum):
    me = lax.axis_index("all")
    node, zq, zp, core = me >> 4, (me >> 2) & 3, (me >> 1) & 1, me & 1
    ids = lookups.T
    core_arg = core.reshape(1)
    turned = ((me >> 1) + 7) & 7
    place = jnp.stack([node, zq, turned >> 1, turned & 1, core])

    def in_hbm(array):
        return pltpu.with_memory_space_constraint(array, pltpu.HBM)

    def flip(array, mask, other=None):
        masks = (mask, mask if other is None else other)
        return lax.ppermute(array, "all", [(i, i ^ masks[i & 1]) for i in range(OWNERS)])

    def exchange(array, groups):
        return lax.all_to_all(array, "all", 0, 0, axis_index_groups=groups, tiled=True)

    def turned_flip(array, mask, other=None):
        masks = (mask, mask if other is None else other)

        def partner(i):
            return (i & ~14) | (((((((i >> 1) + 7) & 7) ^ masks[i & 1]) + 1) & 7) << 1)

        return lax.ppermute(array, "all", [(i, partner(i)) for i in range(OWNERS)])

    with_pair = [
        [n * LOCALS + q * 4 + p * 2 + c for n in reversed(range(NODES)) for p in reversed(range(ZP))] for q in range(ZQ) for c in range(2)
    ]
    by_node = [[n * LOCALS + low for n in range(NODES)] for low in range(LOCALS)]
    alone = [
        [n * LOCALS + low for n in reversed(range(NODES))] for low in range(LOCALS)
    ]
    halves = shape(NODES, ZP, CHUNK, WIDE)
    half_w1, half_hot = (NODES, ZP, CHUNK, PCOL), (NODES, ZP, CHUNK, 2 * E)
    w1_send, w1_own, pre, weights, hits = call(
        backprop_kernel,
        (
            pltpu.VMEM(half_w1, BF),
            pltpu.VMEM(half_w1, BF),
            pltpu.VMEM((TOK, HID), BF),
            pltpu.VMEM((FEAT, HID), BF),
            pltpu.VMEM((TABLES, HOT, TOK), BF),
        ),
        (core_arg, *map(in_hbm, (pooled, ids, converted.reshape(1, TOK), w_hidden, w_out.reshape(HID // E, E)))),
        scalars=1,
        scratch=[
            pltpu.VMEM((TOK, HID), F32),
            pltpu.VMEM((FEAT, TOK), BF),
            pltpu.VMEM((TOK, FEAT), BF),
            pltpu.VMEM((TABLES, TOK), jnp.int32),
            pltpu.VMEM((1, TOK), jnp.int32),
            pltpu.VMEM((HID // E, E), BF),
            pltpu.SemaphoreType.DMA((HID // 256 + 4,)),
        ],
        spec=HBM,
        out_specs=(VMEM,) * 5,
        limit=24,
        flops=3 * 10**9,
        size=8 * MIB,
    )
    w1_far = flip(w1_send, 1)
    hot_send, hot_own, grads = call(
        hot_kernel,
        (pltpu.VMEM(half_hot, BF), pltpu.VMEM(half_hot, BF), shape(TOK, FEAT)),
        (core_arg, pre, weights, hits),
        scalars=1,
        flops=2 * 10**9,
        size=6 * MIB,
    )
    hot_far = flip(hot_send, 1)
    chip = add_part(w1_own, w1_far, 0)
    chip = add_part(hot_own, hot_far, PCOL, chip)
    parts = exchange(chip.reshape(GROUP, CHUNK, WIDE), with_pair)
    cold_send, cold_own = call(
        pack_kernel,
        (shape(SLOT_HALF + NODES, E), shape(SLOT_HALF + NODES, E)),
        (core_arg, ids, grads),
        scalars=1,
        scratch=[pltpu.VMEM((TABLES * TOK, E), BF)],
        flops=6 * 10**9,
        size=8 * MIB,
    )
    cold_keep, cold_give = call(
        cold_split_kernel,
        (shape(NODES + 1, ZQ, PAIR, E), shape(NODES + 1, ZQ, PAIR, E)),
        (place, cold_own, flip(cold_send, 1)),
        scalars=1,
        scratch=[pltpu.VMEM((NODES, ZP, ZQ, PAIR, E), BF)],
        size=2 * MIB,
    )
    slab = call(
        cold_merge_kernel,
        shape(NODES, SLAB, PAIR, E),
        (place, cold_keep, turned_flip(cold_give, 1)),
        scalars=1,
        size=2 * MIB,
    )
    block = ((core * ZP + 1 - zp) * 2 * HALF + (NODES - 1 - node) * CHUNK) // CHUNK
    accum = pick(jnp.stack([block, block + HALF // CHUNK]), in_hbm(hot_accum.reshape(TABLES * HOT, E)))
    slab, accum = lax.optimization_barrier((slab, accum))
    part = call(group_sum_kernel, shape(CHUNK, WIDE), (parts,), size=2 * MIB)
    slab = exchange(slab, by_node)
    quad = [part] + [flip(part, 4 * d, 4 * e) for d, e in zip((2, 1, 3), (3, 2, 1))]
    cold = call(
        cold_dense_kernel,
        tuple(shape(TABLES * COLD_DEV, E) for _ in range(ZQ)),
        (place, slab),
        scalars=1,
        flops=10**9,
        size=2 * MIB,
    )
    quad, cold = lax.optimization_barrier((quad, cold))
    done = call(step_kernel, pltpu.VMEM((CHUNK, WIDE), BF), (*quad, accum))
    beside = flip(done, 2)
    whole = spread(1 - zp.reshape(1), done)
    whole = spread(zp.reshape(1), beside, (whole,))
    half = exchange(whole, alone)
    cold = [cold[0]] + [
        turned_flip(cold[k], 2 * COLD_ORDER[0][k], 2 * COLD_ORDER[1][k]) for k in range(1, ZQ)
    ]
    half, cold = lax.optimization_barrier((half, cold))
    cold_step = call(
        cold_step_kernel,
        shape(TABLES * COLD_DEV, E, dtype=F32),
        (cold_accum.reshape(TABLES * COLD_DEV, E), *cold),
        size=MIB,
    )
    far = flip(half, 1)
    held = finish(core_arg, half)
    w1_grad, hot_step = finish(1 - core_arg, far, held)
    return (w1_grad, hot_step.reshape(TABLES, HOT, E), cold_step.reshape(TABLES, COLD_DEV, E))


def solution(mesh):
    mesh = Mesh(mesh.devices.reshape(OWNERS), ("all",))
    rows = P("all")
    in_specs = (rows, rows, rows, P(), P(), P(), P(None, "all"))
    out_specs = (P(), P(), P(None, "all"))
    return jax.shard_map(on_device, mesh=mesh, in_specs=in_specs, out_specs=out_specs, check_vma=False)
```
